512 devices in a mesh: section: 4 (over z_hi, core), dp: 16 (over x, y), tensor: 8 (over z_lo).
Axes of the slice: x: 4, y: 4, z: 16 (z_hi: 2, z_lo: 8; z = z_hi * 8 + z_lo), core: 2. Of those that a mesh axis runs over, the one named last changes fastest.
Arguments:
- hidden_state_matrix: bfloat16 [4, 2048, 4096], P('section', 'dp', 'tensor'), may hold values from -6 to 6
- specialist_choice_ids: int32 [4, 2048, 8], P('section', 'dp'), may hold values from 0 to 15, as said below
- seat_quota_per_specialist: int32 [4, 16], P('section'), may hold values from 8 to 16, as said below
- candidate_active_extent: int32 [4, 16], P('section', 'dp'), may hold values from 16 to 128, as said below
- normalizer_gain_vector: bfloat16 [4, 4096], P('section'), may hold values from 0.5 to 1.5
- dispatcher_matrix: bfloat16 [4, 16, 4096], P('section'), may hold values from -0.09375 to 0.09375
- gating_matrices: bfloat16 [4, 16, 1536, 4096], P('section', 'dp', 'tensor'), may hold values from -0.09375 to 0.09375
- expanding_matrices: bfloat16 [4, 16, 1536, 4096], P('section', 'dp', 'tensor'), may hold values from -0.09375 to 0.09375
- contracting_matrices: bfloat16 [4, 16, 1536, 4096], P('section', 'dp', None, 'tensor'), may hold values from -0.15625 to 0.15625
Outputs:
- handed: bfloat16 [4, 2048, 4096], P('section', 'dp', 'tensor')
The draws below stay inside these ranges and needn't reach their ends.
Inputs may be any that keep to these rules, and one draw needn't show every extreme that they name: `specialist_choice_ids`: each row names 8 different experts. In each section one expert is named by every row. `seat_quota_per_specialist`: the expert that every row of a section names has capacity 16 there. `candidate_active_extent`: each section has a sequence of 128 live positions.
All inputs are finite; a program needn't handle non-finite values.
Results may differ from the reference program's by a relative error of at most 0.002.
Values may be sent and summed in bfloat16 or wider, within the bound.
No kernel may reach another device: no remote copies, remote signals or barrier semaphores. Data moves between devices by JAX's collectives and lax.ppermute only.
A program may use at most 64 MiB of HBM per device.

```python
import jax
import jax.numpy as jnp
from jax import lax

D = 4096
HID = 1536
TOK_DEV = 128
CAP = 16
EXPERTS = 16
TOP = 8
TOKENS = 2048
N_SECTION = 4
N_DP = 16


def favored_expert(key):
    return jax.random.randint(jax.random.fold_in(key, 101), (N_SECTION,), 0, EXPERTS)


def draw_specialist_choice_ids(key, part):
    favored = favored_expert(key)
    key = jax.random.fold_in(key, 1)
    first_key, second_key = jax.random.split(key)
    noise = jax.random.randint(first_key, (N_SECTION, TOKENS, EXPERTS), 0, 65536)
    leaning = jax.random.randint(second_key, (N_SECTION, 1, EXPERTS), 0, 65536)
    expert_iota = lax.broadcasted_iota(jnp.int32, (N_SECTION, TOKENS, EXPERTS), 2)
    boost = (expert_iota == favored[:, None, None]).astype(jnp.int32) * 4194304
    scores = (noise + leaning + boost) * 32 + expert_iota
    _, chosen = lax.top_k(scores, TOP)
    return chosen.astype(jnp.int32)


def draw_seat_quota_per_specialist(key, part):
    favored = favored_expert(key)
    key = jax.random.fold_in(key, 2)
    extent_bounds = jax.random.randint(key, (N_SECTION, EXPERTS), CAP // 2, CAP + 1)
    expert_iota = lax.broadcasted_iota(jnp.int32, (N_SECTION, EXPERTS), 1)
    return jnp.where(expert_iota == favored[:, None], CAP, extent_bounds).astype(jnp.int32)


def draw_candidate_active_extent(key, part):
    key = jax.random.fold_in(key, 3)
    first_key, second_key = jax.random.split(key)
    lengths = jax.random.randint(first_key, (N_SECTION, N_DP), CAP, TOK_DEV + 1)
    longest = jax.random.randint(second_key, (N_SECTION, 1), 0, N_DP)
    block_iota = lax.broadcasted_iota(jnp.int32, (N_SECTION, N_DP), 1)
    return jnp.where(block_iota == longest, TOK_DEV, lengths).astype(jnp.int32)


def block_scale(key, shape, cuts, low, high):
    def one(axis_at, parts):
        heights = jax.random.uniform(jax.random.fold_in(jax.random.fold_in(key, 6), axis_at), (parts,), jnp.float32, low / len(cuts), high / len(cuts))
        return jnp.repeat(jnp.exp(heights), shape[axis_at] // parts).reshape((-1,) + (1,) * (len(shape) - axis_at - 1))

    level = one(*cuts[0])
    for cut in cuts[1:]:
        level = level * one(*cut)
    return level


def bell_draw(own_key, shape, spread, bound, shards=(), kind=jnp.bfloat16):
    entries = spread * jax.random.normal(own_key, shape, jnp.float32)
    if shards:
        entries = entries * block_scale(own_key, shape, shards, -0.22, 0.18)
    return jnp.clip(entries, -bound, bound).astype(kind)


def setup_inputs(seed: int = 0) -> dict:
    streams_of = jax.random.split(jax.random.key(seed), 10)
    hidden_state_matrix = bell_draw(streams_of[0], (N_SECTION, TOKENS, D), 1.0, 6.0, ((0, 4), (1, 16), (2, 8)))
    specialist_choice_ids = draw_specialist_choice_ids(jax.random.fold_in(streams_of[9], 71), 0)
    seat_quota_per_specialist = draw_seat_quota_per_specialist(jax.random.fold_in(streams_of[9], 71), 0)
    candidate_active_extent = draw_candidate_active_extent(jax.random.fold_in(streams_of[9], 71), 0)
    normalizer_gain_vector = jnp.clip(1.0 + 0.1 * jax.random.normal(streams_of[4], (N_SECTION, D), jnp.float32), 0.5, 1.5).astype(jnp.bfloat16)
    dispatcher_matrix = bell_draw(streams_of[5], (N_SECTION, EXPERTS, D), D ** -0.5, 0.09375, ((0, 4),))
    gating_matrices = bell_draw(streams_of[6], (N_SECTION, EXPERTS, HID, D), D ** -0.5, 0.09375, ((0, 4), (1, 16), (2, 8)))
    expanding_matrices = bell_draw(streams_of[7], (N_SECTION, EXPERTS, HID, D), D ** -0.5, 0.09375, ((0, 4), (1, 16), (2, 8)))
    contracting_matrices = bell_draw(streams_of[8], (N_SECTION, EXPERTS, HID, D), HID ** -0.5, 0.15625, ((0, 4), (1, 16), (3, 8)))
    return dict(hidden_state_matrix=hidden_state_matrix, specialist_choice_ids=specialist_choice_ids, seat_quota_per_specialist=seat_quota_per_specialist, candidate_active_extent=candidate_active_extent, normalizer_gain_vector=normalizer_gain_vector, dispatcher_matrix=dispatcher_matrix, gating_matrices=gating_matrices, expanding_matrices=expanding_matrices, contracting_matrices=contracting_matrices)


norm_eps = 1e-06

def against_rows(left, right):
    return lax.dot_general(left, right, (((1,), (1,)), ((), ())), preferred_element_type=jnp.float32)

def routing_tables(routes, lengths, extent_bounds):
    expert_iota = lax.broadcasted_iota(jnp.int32, (1, 1, EXPERTS), 2)
    chosen = lax.optimization_barrier(jnp.sum((routes.astype(jnp.int32)[:, :, None] == expert_iota).astype(jnp.int32), axis=1))
    blocked = chosen.reshape(N_DP, TOK_DEV, EXPERTS)
    row_iota = lax.broadcasted_iota(jnp.int32, (N_DP, TOK_DEV, 1), 1)
    live = (row_iota < lengths.astype(jnp.int32)[:, None, None]).astype(jnp.int32)
    picked = blocked * live
    order = jnp.cumsum(picked, axis=1) - picked
    kept = picked * (order < extent_bounds.astype(jnp.int32)[None, None, :]).astype(jnp.int32)
    return (chosen, order, kept)

def segment_specialist_block(tokens, routes, extent_bounds, lengths, gain, router_rows, gates, uppers, downs):
    widened = tokens.astype(jnp.float32)
    inverse = lax.rsqrt(lax.optimization_barrier(jnp.mean(widened * widened, axis=1, keepdims=True)) + norm_eps)
    normed = (widened * inverse * gain.astype(jnp.float32)[None, :]).astype(jnp.bfloat16)
    logits = against_rows(normed, router_rows)
    chosen, order, kept = routing_tables(routes, lengths, extent_bounds)
    powered = jnp.exp(logits) * chosen.astype(jnp.float32)
    weight = powered / lax.optimization_barrier(jnp.sum(powered, axis=1, keepdims=True))
    slot_iota = lax.broadcasted_iota(jnp.int32, (1, 1, CAP), 2)
    row_iota = lax.broadcasted_iota(jnp.int32, (1, TOK_DEV, 1), 1)
    offsets = lax.broadcasted_iota(jnp.int32, (N_DP, 1), 0) * TOK_DEV

    def one_expert(total, inputs):
        w_gate, w_up, w_down, expert = inputs
        kept_e = lax.dynamic_index_in_dim(kept, expert, axis=2, keepdims=False)
        order_e = lax.dynamic_index_in_dim(order, expert, axis=2, keepdims=False)
        match = kept_e[:, :, None] * (order_e[:, :, None] == slot_iota).astype(jnp.int32)
        slot_row = lax.optimization_barrier(jnp.sum(match * row_iota, axis=1)) + offsets
        filled = lax.optimization_barrier(jnp.sum(match, axis=1)).reshape(-1)
        index = slot_row.reshape(-1).astype(jnp.int32)
        rows = jnp.take(normed, index, axis=0)
        gate = against_rows(rows, w_gate)
        upper = against_rows(rows, w_up)
        hidden = (jax.nn.silu(gate) * upper).astype(jnp.bfloat16)
        projected = jnp.dot(hidden, w_down, preferred_element_type=jnp.float32)
        weight_e = lax.dynamic_index_in_dim(weight, expert, axis=1, keepdims=False)
        picked_weight = jnp.take(weight_e, index, axis=0)
        rounded = (projected * picked_weight[:, None]).astype(jnp.bfloat16)
        rounded = lax.optimization_barrier(rounded)
        contribution = jnp.where(filled[:, None] > 0, rounded.astype(jnp.float32), jnp.zeros((), jnp.float32))
        return (total.at[index].add(contribution), None)
    start = jnp.zeros((TOKENS, D), jnp.float32)
    experts_iota = jnp.arange(EXPERTS, dtype=jnp.int32)
    total, _ = lax.scan(one_expert, start, (gates, uppers, downs, experts_iota))
    return (widened + total).astype(jnp.bfloat16)

def reference(hidden_state_matrix, specialist_choice_ids, seat_quota_per_specialist, candidate_active_extent, normalizer_gain_vector, dispatcher_matrix, gating_matrices, expanding_matrices, contracting_matrices):
    specialist_result_vectors = []
    for handover_segment in range(N_SECTION):
        specialist_result_vectors.append(segment_specialist_block(hidden_state_matrix[handover_segment], specialist_choice_ids[handover_segment], seat_quota_per_specialist[handover_segment], candidate_active_extent[handover_segment], normalizer_gain_vector[handover_segment], dispatcher_matrix[handover_segment], gating_matrices[handover_segment], expanding_matrices[handover_segment], contracting_matrices[handover_segment]))
    stacked = jnp.stack(specialist_result_vectors, axis=0)
    return jnp.roll(stacked, 1, axis=0)
```

```python
import jax
import jax.numpy as jnp
from jax import lax
from jax.experimental import pallas as pl
from jax.experimental.pallas import tpu as pltpu
from jax.sharding import PartitionSpec as P

norm_eps = 1e-06
BF = jnp.bfloat16
F32 = jnp.float32
EXPERTS = 16
SLOTS = 16
VM = pl.BlockSpec(memory_space=pltpu.VMEM)
SM = pl.BlockSpec(memory_space=pltpu.SMEM)
FOURS = [[0, 1, 2, 3], [4, 5, 6, 7]]


def dot(a, b, da, db):
    return lax.dot_general(a, b, (((da,), (db,)), ((), ())), preferred_element_type=F32)


def call(body, shape, specs, args, flops=0, moved=0, limit=24):
    return pl.pallas_call(
        body,
        out_shape=shape,
        in_specs=specs,
        out_specs=jax.tree.map(lambda _: VM, shape),
        compiler_params=pltpu.CompilerParams(vmem_limit_bytes=limit * 2**20),
        cost_estimate=pl.CostEstimate(flops=flops, bytes_accessed=moved, transcendentals=0),
    )(*args)


def choices(ids):
    expert = lax.broadcasted_iota(jnp.int32, (EXPERTS, ids.shape[1]), 0)
    total = jnp.zeros(expert.shape, F32)
    for j in range(ids.shape[0]):
        total = total + (ids[j : j + 1, :] == expert).astype(F32)
    return total


def route_body(length_ref, ids_ref, quota_ref, match_ref):
    n = ids_ref.shape[1]
    at = lax.broadcasted_iota(jnp.int32, (1, n), 1)
    picked = choices(ids_ref[...]) * (at < length_ref[0]).astype(F32)
    before = (
        lax.broadcasted_iota(jnp.int32, (n, n), 0) < lax.broadcasted_iota(jnp.int32, (n, n), 1)
    ).astype(BF)
    order = dot(picked.astype(BF), before, 1, 0)
    kept = picked * (order < quota_ref[...].astype(F32)).astype(F32)
    slot = lax.broadcasted_iota(jnp.int32, (SLOTS, n), 0).astype(F32)
    for e in range(EXPERTS):
        hit = (order[e : e + 1, :] == slot).astype(F32) * kept[e : e + 1, :]
        match_ref[e * SLOTS : (e + 1) * SLOTS, :] = hit.astype(BF)


def pick_body(match_ref, rows_ref, out_ref):
    parts, _, width = rows_ref.shape
    for k in range(parts):
        out_ref[:, k * width : (k + 1) * width] = dot(match_ref[...], rows_ref[k], 1, 0).astype(BF)


def weigh_body(half_ref, first_ref, second_ref, gain_ref, router_ref, ids_ref, match_ref, high_ref, low_ref):
    parts, n, width = first_ref.shape
    full = 2 * parts * width
    squares = jnp.zeros((n, 1), F32)
    for ref in (first_ref, second_ref):
        for k in range(parts):
            v = ref[k].astype(F32)
            squares = squares + jnp.sum(v * v, axis=1, keepdims=True)
    inverse = lax.rsqrt(squares / full + norm_eps)
    logits = jnp.zeros((EXPERTS, n), F32)
    for ref, half in ((first_ref, half_ref[0]), (second_ref, 1 - half_ref[0])):
        for k in range(parts):
            cols = pl.ds(pl.multiple_of((half * parts + k) * width, width), width)
            normed = (ref[k].astype(F32) * inverse * gain_ref[:, cols].astype(F32)).astype(BF)
            logits = logits + dot(router_ref[:, cols], normed, 1, 1)
    powered = jnp.exp(logits) * choices(ids_ref[...])
    weight = powered / jnp.sum(powered, axis=0, keepdims=True)
    for e in range(EXPERTS):
        rows = slice(e * SLOTS, (e + 1) * SLOTS)
        value = match_ref[rows, :].astype(F32) * weight[e : e + 1, :]
        high = value.astype(BF)
        high_ref[rows, :] = high
        low_ref[rows, :] = (value - high.astype(F32)).astype(BF)


def expand_body(half_ref, first_ref, second_ref, gain_ref, gate_ref, up_ref, out_ref):
    rows, span = first_ref.shape
    step = 512
    squares = jnp.zeros((rows, 1), F32)
    for ref in (first_ref, second_ref):
        for k in range(span // step):
            v = ref[:, k * step : (k + 1) * step].astype(F32)
            squares = squares + jnp.sum(v * v, axis=1, keepdims=True)
    inverse = lax.rsqrt(squares / (2 * span) + norm_eps)
    hid = gate_ref.shape[0]
    gate = jnp.zeros((hid, rows), F32)
    up = jnp.zeros((hid, rows), F32)
    for ref, half in ((first_ref, half_ref[0]), (second_ref, 1 - half_ref[0])):
        for k in range(span // step):
            cols = pl.ds(pl.multiple_of(half * span + k * step, step), step)
            v = ref[:, k * step : (k + 1) * step].astype(F32)
            normed = (v * inverse * gain_ref[:, cols].astype(F32)).astype(BF)
            gate = gate + dot(gate_ref[:, cols], normed, 1, 1)
            up = up + dot(up_ref[:, cols], normed, 1, 1)
    out_ref[...] = (gate / (1.0 + jnp.exp(-gate)) * up).astype(BF)


def contract_body(half_ref, first_ref, second_ref, down_ref, out_ref):
    parts, hid, _ = first_ref.shape
    total = jnp.zeros(out_ref.shape, F32)
    for ref, half in ((first_ref, half_ref[0]), (second_ref, 1 - half_ref[0])):
        for k in range(parts):
            rows = pl.ds(pl.multiple_of((half * parts + k) * hid, hid), hid)
            total = total + dot(ref[k], down_ref[rows, :], 0, 0)
    out_ref[...] = total.astype(BF)


def mix_body(high_ref, low_ref, reply_ref, tokens_ref, out_ref):
    mixed = dot(high_ref[...], reply_ref[...], 0, 0) + dot(low_ref[...], reply_ref[...], 0, 0)
    out_ref[...] = (tokens_ref[...].astype(F32) + mixed).astype(BF)


def to_fours(shard):
    copies = jnp.broadcast_to(shard[None], (4,) + shard.shape)
    return lax.all_to_all(copies, "tensor", 0, 0, axis_index_groups=FOURS)


def across(shard):
    return lax.ppermute(shard, "tensor", [(i, i ^ 4) for i in range(8)])


def over_dp(rows):
    n, width = rows.shape
    return lax.all_to_all(rows.reshape(EXPERTS, n // EXPERTS, width), "dp", 0, 0).reshape(n, width)


def on_device(
    hidden_state_matrix,
    specialist_choice_ids,
    seat_quota_per_specialist,
    candidate_active_extent,
    normalizer_gain_vector,
    dispatcher_matrix,
    gating_matrices,
    expanding_matrices,
    contracting_matrices,
):
    tokens = hidden_state_matrix[0]
    ids = specialist_choice_ids[0].T
    quota = seat_quota_per_specialist[0][:, None]
    length = candidate_active_extent[0]
    gain = normalizer_gain_vector
    router = dispatcher_matrix[0]
    w_gate = gating_matrices[0, 0]
    w_up = expanding_matrices[0, 0]
    w_down = contracting_matrices[0, 0]
    n, width = tokens.shape
    slots = EXPERTS * SLOTS
    hid = w_gate.shape[0]
    half = (lax.axis_index("tensor") // 4).astype(jnp.int32)[None]

    other = across(tokens)
    first = to_fours(tokens)
    match = call(route_body, jax.ShapeDtypeStruct((slots, n), BF), [SM, VM, VM], (length, ids, quota))
    out_rows = jax.ShapeDtypeStruct((slots, 4 * width), BF)
    first_rows = over_dp(call(pick_body, out_rows, [VM] * 2, (match, first)))
    second = to_fours(other)
    second_rows = over_dp(call(pick_body, out_rows, [VM] * 2, (match, second)))
    pair = jax.ShapeDtypeStruct((slots, n), BF)
    high, low = call(
        weigh_body, (pair, pair), [SM] + [VM] * 6, (half, first, second, gain, router, ids, match)
    )
    hidden = call(
        expand_body,
        jax.ShapeDtypeStruct((hid, slots), BF),
        [SM] + [VM] * 5,
        (half, first_rows, second_rows, gain, w_gate, w_up),
    )
    hidden_other = across(hidden)
    hidden_first = to_fours(hidden)
    hidden_second = to_fours(hidden_other)
    reply = call(
        contract_body,
        jax.ShapeDtypeStruct((slots, width), BF),
        [SM] + [VM] * 3,
        (half, hidden_first, hidden_second, w_down),
    )
    returned = over_dp(reply)
    layer_out = call(
        mix_body, jax.ShapeDtypeStruct((n, width), BF), [VM] * 4, (high, low, returned, tokens)
    )
    count = lax.axis_size("section")
    handed = lax.ppermute(layer_out, "section", [(i, (i + 1) % count) for i in range(count)])
    return handed[None]


def solution(mesh):
    return jax.shard_map(
        on_device,
        mesh=mesh,
        in_specs=(
            P("section", "dp", "tensor"),
            P("section", "dp", None),
            P("section", None),
            P("section", "dp"),
            P("section", None),
            P("section", None, None),
            P("section", "dp", "tensor", None),
            P("section", "dp", "tensor", None),
            P("section", "dp", None, "tensor"),
        ),
        out_specs=P("section", "dp", "tensor"),
        check_vma=False,
    )
```

```python
import jax
import jax.numpy as jnp
from jax import lax
from jax.experimental import pallas as pl
from jax.experimental.pallas import tpu as pltpu
from jax.sharding import PartitionSpec as P

norm_eps = 1e-06
BF = jnp.bfloat16
F32 = jnp.float32
EXPERTS = 16
SLOTS = 16
VM = pl.BlockSpec(memory_space=pltpu.VMEM)
SM = pl.BlockSpec(memory_space=pltpu.SMEM)
HB = pl.BlockSpec(memory_space=pltpu.HBM)
FOURS = [[0, 1, 2, 3], [4, 5, 6, 7]]


def dot(a, b, da, db):
    return lax.dot_general(a, b, (((da,), (db,)), ((), ())), preferred_element_type=F32)


def call(body, shape, specs, args, scratch=(), flops=0, moved=0, limit=24):
    return pl.pallas_call(
        body,
        scratch_shapes=list(scratch),
        out_shape=shape,
        in_specs=specs,
        out_specs=jax.tree.map(lambda _: VM, shape),
        compiler_params=pltpu.CompilerParams(vmem_limit_bytes=limit * 2**20),
        cost_estimate=pl.CostEstimate(flops=flops, bytes_accessed=moved, transcendentals=0),
    )(*args)


def choices(ids):
    expert = lax.broadcasted_iota(jnp.int32, (EXPERTS, ids.shape[1]), 0)
    total = jnp.zeros(expert.shape, F32)
    for j in range(ids.shape[0]):
        total = total + (ids[j : j + 1, :] == expert).astype(F32)
    return total


def route_body(length_ref, ids_ref, quota_ref, match_ref):
    n = ids_ref.shape[1]
    at = lax.broadcasted_iota(jnp.int32, (1, n), 1)
    picked = choices(ids_ref[...]) * (at < length_ref[0]).astype(F32)
    before = (
        lax.broadcasted_iota(jnp.int32, (n, n), 0) < lax.broadcasted_iota(jnp.int32, (n, n), 1)
    ).astype(BF)
    order = dot(picked.astype(BF), before, 1, 0)
    kept = picked * (order < quota_ref[...].astype(F32)).astype(F32)
    slot = lax.broadcasted_iota(jnp.int32, (SLOTS, n), 0).astype(F32)
    for e in range(EXPERTS):
        hit = (order[e : e + 1, :] == slot).astype(F32) * kept[e : e + 1, :]
        match_ref[e * SLOTS : (e + 1) * SLOTS, :] = hit.astype(BF)


def blocks_of(rank, half, width):
    order = [half * 4 + k for k in range(4)] + [rank ^ 4 ^ k for k in range(4)]
    return [pl.ds(pl.multiple_of(r * width, width), width) for r in order]


def pick_first_body(match_ref, group_ref, other_ref, out_ref):
    parts, _, width = group_ref.shape
    for k in range(parts):
        out_ref[:, k * width : (k + 1) * width] = dot(match_ref[...], group_ref[k], 1, 0).astype(BF)
    out_ref[:, parts * width :] = dot(match_ref[...], other_ref[...], 1, 0).astype(BF)


def pick_second_body(match_ref, *refs):
    *rows_refs, out_ref = refs
    width = rows_refs[0].shape[1]
    for k, ref in enumerate(rows_refs):
        out_ref[:, k * width : (k + 1) * width] = dot(match_ref[...], ref[...], 1, 0).astype(BF)


def weigh_body(group_ref, a_ref, b_ref, c_ref, d_ref, gain_ref, router_ref, ids_ref, match_ref, high_ref, low_ref):
    n, width = a_ref.shape
    rank = lax.axis_index("tensor")
    blocks = blocks_of(rank, rank // 4, width)
    views = [group_ref.at[k] for k in range(4)] + [a_ref, b_ref, c_ref, d_ref]
    squares = jnp.zeros((n, 1), F32)
    for view in views:
        v = view[...].astype(F32)
        squares = squares + jnp.sum(v * v, axis=1, keepdims=True)
    inverse = lax.rsqrt(squares / (8 * width) + norm_eps)
    logits = jnp.zeros((EXPERTS, n), F32)
    for view, cols in zip(views, blocks):
        normed = (view[...].astype(F32) * inverse * gain_ref[:, cols].astype(F32)).astype(BF)
        logits = logits + dot(router_ref[:, cols], normed, 1, 1)
    powered = jnp.exp(logits) * choices(ids_ref[...])
    weight = powered / jnp.sum(powered, axis=0, keepdims=True)
    for e in range(EXPERTS):
        rows = slice(e * SLOTS, (e + 1) * SLOTS)
        value = match_ref[rows, :].astype(F32) * weight[e : e + 1, :]
        high = value.astype(BF)
        high_ref[rows, :] = high
        low_ref[rows, :] = (value - high.astype(F32)).astype(BF)


def expand_body(first_ref, second_ref, gain_ref, gate_ref, up_ref, out_ref, gate_buf, up_buf, sems):
    rows = first_ref.shape[0]
    parts, hid, width = gate_buf.shape
    rank = lax.axis_index("tensor")
    blocks = blocks_of(rank, rank // 4, width)
    copies = []
    for k, cols in enumerate(blocks):
        one = pltpu.make_async_copy(gate_ref.at[:, cols], gate_buf.at[k], sems.at[0, k])
        two = pltpu.make_async_copy(up_ref.at[:, cols], up_buf.at[k], sems.at[1, k])
        one.start()
        two.start()
        copies.append((one, two))
    cut = first_ref.shape[1] // width
    views = [first_ref.at[:, k * width : (k + 1) * width] for k in range(cut)]
    views += [second_ref.at[:, k * width : (k + 1) * width] for k in range(parts - cut)]
    squares = jnp.zeros((rows, 1), F32)
    for view in views:
        v = view[...].astype(F32)
        squares = squares + jnp.sum(v * v, axis=1, keepdims=True)
    inverse = lax.rsqrt(squares / (parts * width) + norm_eps)
    gate = jnp.zeros((hid, rows), F32)
    up = jnp.zeros((hid, rows), F32)
    for k, (view, cols) in enumerate(zip(views, blocks)):
        normed = (view[...].astype(F32) * inverse * gain_ref[:, cols].astype(F32)).astype(BF)
        for copy in copies[k]:
            copy.wait()
        gate = gate + dot(gate_buf[k], normed, 1, 1)
        up = up + dot(up_buf[k], normed, 1, 1)
    out_ref[...] = (gate / (1.0 + jnp.exp(-gate)) * up).astype(BF)


def contract_body(half_ref, first_ref, second_ref, down_ref, out_ref):
    parts, hid, _ = first_ref.shape
    total = jnp.zeros(out_ref.shape, F32)
    for ref, half in ((first_ref, half_ref[0]), (second_ref, 1 - half_ref[0])):
        for k in range(parts):
            rows = pl.ds(pl.multiple_of((half * parts + k) * hid, hid), hid)
            total = total + dot(ref[k], down_ref[rows, :], 0, 0)
    out_ref[...] = total.astype(BF)


def mix_body(high_ref, low_ref, reply_ref, tokens_ref, out_ref):
    mixed = dot(high_ref[...], reply_ref[...], 0, 0) + dot(low_ref[...], reply_ref[...], 0, 0)
    out_ref[...] = (tokens_ref[...].astype(F32) + mixed).astype(BF)


def to_fours(shard):
    copies = jnp.broadcast_to(shard[None], (4,) + shard.shape)
    return lax.all_to_all(copies, "tensor", 0, 0, axis_index_groups=FOURS)


def along(shard, by):
    return lax.ppermute(shard, "tensor", [(i, i ^ by) for i in range(8)])


def over_dp(rows):
    n, width = rows.shape
    return lax.all_to_all(rows.reshape(EXPERTS, n // EXPERTS, width), "dp", 0, 0).reshape(n, width)


def on_device(
    hidden_state_matrix,
    specialist_choice_ids,
    seat_quota_per_specialist,
    candidate_active_extent,
    normalizer_gain_vector,
    dispatcher_matrix,
    gating_matrices,
    expanding_matrices,
    contracting_matrices,
):
    tokens = hidden_state_matrix[0]
    ids = specialist_choice_ids[0].T
    quota = seat_quota_per_specialist[0][:, None]
    length = candidate_active_extent[0]
    gain = normalizer_gain_vector
    router = dispatcher_matrix[0]
    w_gate = gating_matrices[0, 0]
    w_up = expanding_matrices[0, 0]
    w_down = contracting_matrices[0, 0]
    n, width = tokens.shape
    slots = EXPERTS * SLOTS
    hid = w_gate.shape[0]
    half = (lax.axis_index("tensor") // 4).astype(jnp.int32)[None]

    other = along(tokens, 4)
    group = to_fours(tokens)
    match = call(route_body, jax.ShapeDtypeStruct((slots, n), BF), [SM, VM, VM], (length, ids, quota))
    first = call(
        pick_first_body, jax.ShapeDtypeStruct((slots, 5 * width), BF), [VM] * 3, (match, group, other)
    )
    first_rows = over_dp(first)
    rest = [along(other, by) for by in (1, 2, 3)]
    second = call(
        pick_second_body, jax.ShapeDtypeStruct((slots, 3 * width), BF), [VM] * 4, (match, *rest)
    )
    first_rows, second = lax.optimization_barrier((first_rows, second))
    second_rows = over_dp(second)
    pair = jax.ShapeDtypeStruct((slots, n), BF)
    high, low = call(
        weigh_body, (pair, pair), [VM] * 9, (group, other, *rest, gain, router, ids, match)
    )
    hidden = call(
        expand_body,
        jax.ShapeDtypeStruct((hid, slots), BF),
        [VM] * 3 + [HB] * 2,
        (first_rows, second_rows, gain, w_gate, w_up),
        [pltpu.VMEM((8, hid, width), BF)] * 2 + [pltpu.SemaphoreType.DMA((2, 8))],
        limit=48,
    )
    hidden_other = along(hidden, 4)
    hidden_first = to_fours(hidden)
    hidden_second = to_fours(hidden_other)
    reply = call(
        contract_body,
        jax.ShapeDtypeStruct((slots, width), BF),
        [SM] + [VM] * 3,
        (half, hidden_first, hidden_second, w_down),
    )
    returned = over_dp(reply)
    layer_out = call(
        mix_body, jax.ShapeDtypeStruct((n, width), BF), [VM] * 4, (high, low, returned, tokens)
    )
    count = lax.axis_size("section")
    handed = lax.ppermute(layer_out, "section", [(i, (i + 1) % count) for i in range(count)])
    return handed[None]


def solution(mesh):
    return jax.shard_map(
        on_device,
        mesh=mesh,
        in_specs=(
            P("section", "dp", "tensor"),
            P("section", "dp", None),
            P("section", None),
            P("section", "dp"),
            P("section", None),
            P("section", None, None),
            P("section", "dp", "tensor", None),
            P("section", "dp", "tensor", None),
            P("section", "dp", None, "tensor"),
        ),
        out_specs=P("section", "dp", "tensor"),
        check_vma=False,
    )
```

```python
import jax
import jax.numpy as jnp
from jax import lax
from jax.experimental import pallas as pl
from jax.experimental.pallas import tpu as pltpu
from jax.sharding import PartitionSpec as P

norm_eps = 1e-06
BF = jnp.bfloat16
F32 = jnp.float32
EXPERTS = 16
SLOTS = 16
VM = pl.BlockSpec(memory_space=pltpu.VMEM)
SM = pl.BlockSpec(memory_space=pltpu.SMEM)
HB = pl.BlockSpec(memory_space=pltpu.HBM)
SIZES = (48, 64, 80, 96, 128)
FOURS = [[0, 1, 2, 3], [4, 5, 6, 7]]


def dot(a, b, da, db):
    return lax.dot_general(a, b, (((da,), (db,)), ((), ())), preferred_element_type=F32)


def call(body, shape, specs, args, scratch=(), out_specs=None, flops=0, moved=0, limit=24):
    return pl.pallas_call(
        body,
        scratch_shapes=list(scratch),
        out_shape=shape,
        in_specs=specs,
        out_specs=out_specs or jax.tree.map(lambda _: VM, shape),
        compiler_params=pltpu.CompilerParams(vmem_limit_bytes=limit * 2**20),
        cost_estimate=pl.CostEstimate(flops=flops, bytes_accessed=moved, transcendentals=0),
    )(*args)


def eye(n):
    return (lax.broadcasted_iota(jnp.int32, (n, n), 0) == lax.broadcasted_iota(jnp.int32, (n, n), 1)).astype(BF)


def route_body(ids_ref, length_ref, quota_ref, tokens_ref, rows_ref, match_ref, held_ref, chosen_ref, which_ref):
    n = ids_ref.shape[1]
    expert = lax.broadcasted_iota(jnp.int32, (EXPERTS, n), 0)
    chosen = jnp.zeros((EXPERTS, n), F32)
    for j in range(ids_ref.shape[0]):
        chosen = chosen + (ids_ref[j : j + 1, :] == expert).astype(F32)
    at = lax.broadcasted_iota(jnp.int32, (1, n), 1)
    picked = chosen * (at < length_ref[...]).astype(F32)
    down = lax.broadcasted_iota(jnp.int32, (n, n), 0)
    before = (down < lax.broadcasted_iota(jnp.int32, (n, n), 1)).astype(BF)
    order = dot(picked.astype(BF), before, 1, 0)
    quota = jnp.sum(eye(EXPERTS).astype(F32) * quota_ref[...].astype(F32), axis=1, keepdims=True)
    kept = picked * (order < quota).astype(F32)
    slot = lax.broadcasted_iota(jnp.int32, (SLOTS, n), 0).astype(F32)
    hits = [(order[e : e + 1, :] == slot).astype(F32) * kept[e : e + 1, :] for e in range(EXPERTS)]
    match = dot(eye(n), jnp.concatenate(hits, axis=0).astype(BF), 1, 1).astype(BF)
    used = jnp.max(kept, axis=0, keepdims=True)
    place = dot(jnp.broadcast_to(used, (8, n)).astype(BF), before, 1, 0)[0:1, :]
    compact = ((place == down.astype(F32)).astype(F32) * used).astype(BF)
    rows_ref[...] = dot(compact, tokens_ref[...], 1, 0).astype(BF)
    match_ref[...] = match
    held_ref[...] = dot(compact, match, 1, 0).astype(BF)
    chosen_ref[...] = dot(compact, chosen.astype(BF), 1, 1)
    count = jnp.sum(used).astype(jnp.int32)
    which_ref[0] = sum((count > size).astype(jnp.int32) for size in SIZES[:-1])


def blocks_of(rank, width):
    order = [rank // 4 * 4 + k for k in range(4)] + [rank ^ 4 ^ k for k in range(4)]
    return [pl.ds(pl.multiple_of(r * width, width), width) for r in order]


def pick(views, blocks, held, gain_ref, router_ref, out_ref):
    n, width = views[0].shape
    squares = jnp.zeros((n, 1), F32)
    logits = jnp.zeros((n, EXPERTS), F32)
    for k, (view, cols) in enumerate(zip(views, blocks)):
        raw = view[...]
        out_ref[:, k * width : (k + 1) * width] = dot(held, raw, 0, 0).astype(BF)
        v = raw.astype(F32)
        squares = squares + jnp.sum(v * v, axis=1, keepdims=True)
        scaled = (v * gain_ref[:, cols].astype(F32)).astype(BF)
        logits = logits + dot(scaled, router_ref[:, cols], 1, 1)
    return squares, logits


def pick_first_body(own_ref, far_ref, held_ref, gain_ref, router_ref, out_ref, kept_far_ref, squares_ref, logits_ref):
    n, width = far_ref.shape
    blocks = blocks_of(lax.axis_index("tensor"), width)[:5]
    views = [own_ref.at[k] for k in range(4)] + [far_ref]
    squares, logits = pick(views, blocks, held_ref[0:n, :], gain_ref, router_ref, out_ref)
    kept_far_ref[0:n, :] = far_ref[...]
    squares_ref[0:n, :] = jnp.broadcast_to(squares, (n, squares_ref.shape[1]))
    logits_ref[0:n, :] = logits


def pick_second_body(
    a_ref, b_ref, c_ref, held_ref, gain_ref, router_ref, squares_ref, logits_ref, match_ref, chosen_ref,
    out_ref, high_ref, low_ref,
):
    n, width = a_ref.shape
    blocks = blocks_of(lax.axis_index("tensor"), width)[5:]
    held = held_ref[0:n, :]
    squares, logits = pick([a_ref, b_ref, c_ref], blocks, held, gain_ref, router_ref, out_ref)
    inverse = lax.rsqrt((squares + squares_ref[0:n, 0:1]) / (8 * width) + norm_eps)
    chosen = chosen_ref[0:n, :]
    powered = jnp.exp((logits + logits_ref[0:n, :]) * inverse) * chosen
    weight = powered / (jnp.sum(powered, axis=1, keepdims=True) + (1.0 - jnp.max(chosen, axis=1, keepdims=True)))
    slots = held.shape[1]
    owner = (
        lax.broadcasted_iota(jnp.int32, (EXPERTS, slots), 1) // SLOTS
        == lax.broadcasted_iota(jnp.int32, (EXPERTS, slots), 0)
    ).astype(BF)
    spread = jnp.zeros((n, slots), F32)
    for _ in range(3):
        piece = weight.astype(BF)
        spread = spread + dot(piece, owner, 1, 0)
        weight = weight - piece.astype(F32)
    row = jnp.sum(spread * held.astype(F32), axis=0, keepdims=True)
    value = match_ref[...].astype(F32) * row
    high = value.astype(BF)
    high_ref[...] = high
    low_ref[...] = (value - high.astype(F32)).astype(BF)


def partial_products(rows_ref, gain_ref, blocks, weights):
    rows = rows_ref.shape[0]
    squares = jnp.zeros((rows, 1), F32)
    gate = up = 0.0
    for k, cols in enumerate(blocks):
        width = rows_ref.shape[1] // len(blocks)
        v = rows_ref[:, k * width : (k + 1) * width].astype(F32)
        squares = squares + jnp.sum(v * v, axis=1, keepdims=True)
        scaled = (v * gain_ref[:, cols].astype(F32)).astype(BF)
        gate_part, up_part = weights(k)
        gate = gate + dot(gate_part, scaled, 1, 1)
        up = up + dot(up_part, scaled, 1, 1)
    return gate, up, jnp.broadcast_to(squares, (rows, 128)).T[0:1, :]


def expand_first_body(
    rows_ref, gain_ref, gate_ref, up_ref,
    parts_ref, gate_rest, up_rest, gate_buf, up_buf, sems,
):
    rank = lax.axis_index("tensor")
    now, _, width = gate_buf.shape
    blocks = blocks_of(rank, width)
    copies = []
    for k, cols in enumerate(blocks):
        targets = (gate_buf, up_buf) if k < now else (gate_rest, up_rest)
        at = k if k < now else k - now
        pair = [
            pltpu.make_async_copy(source.at[:, cols], target.at[at], sems.at[i, k])
            for i, (source, target) in enumerate(zip((gate_ref, up_ref), targets))
        ]
        for copy in pair:
            copy.start()
        copies.append(pair)

    def weights(k):
        for copy in copies[k]:
            copy.wait()
        return gate_buf[k], up_buf[k]

    gate, up, squares = partial_products(rows_ref, gain_ref, blocks[:now], weights)
    hid, rows = gate.shape
    parts_ref[0:hid, :] = gate
    parts_ref[hid : 2 * hid, :] = up
    parts_ref[2 * hid :, :] = jnp.broadcast_to(squares, (8, rows))
    for pair in copies[now:]:
        for copy in pair:
            copy.wait()


def expand_second_body(rows_ref, parts_ref, gain_ref, gate_rest, up_rest, out_ref):
    rank = lax.axis_index("tensor")
    parts, hid, width = gate_rest.shape
    blocks = blocks_of(rank, width)[8 - parts :]
    gate, up, squares = partial_products(
        rows_ref, gain_ref, blocks, lambda k: (gate_rest[k], up_rest[k])
    )
    inverse = lax.rsqrt((squares + parts_ref[2 * hid : 2 * hid + 1, :]) / (8 * width) + norm_eps)
    gate = (gate + parts_ref[0:hid, :]) * inverse
    up = (up + parts_ref[hid : 2 * hid, :]) * inverse
    out_ref[...] = (gate / (1.0 + jnp.exp(-gate)) * up).astype(BF)


def contract_body(half_ref, first_ref, second_ref, down_ref, out_ref):
    parts, hid, _ = first_ref.shape
    total = jnp.zeros(out_ref.shape, F32)
    for ref, half in ((first_ref, half_ref[0]), (second_ref, 1 - half_ref[0])):
        for k in range(parts):
            rows = pl.ds(pl.multiple_of((half * parts + k) * hid, hid), hid)
            total = total + dot(ref[k], down_ref[rows, :], 0, 0)
    out_ref[...] = total.astype(BF)


def mix_body(high_ref, low_ref, reply_ref, tokens_ref, out_ref):
    mixed = dot(high_ref[...], reply_ref[...], 1, 0) + dot(low_ref[...], reply_ref[...], 1, 0)
    out_ref[...] = (tokens_ref[...].astype(F32) + mixed).astype(BF)


def to_fours(shard):
    copies = jnp.broadcast_to(shard[None], (4,) + shard.shape)
    return lax.all_to_all(copies, "tensor", 0, 0, axis_index_groups=FOURS)


def along(shard, by):
    return lax.ppermute(shard, "tensor", [(i, i ^ by) for i in range(8)])


def over_dp(rows):
    n, width = rows.shape
    return lax.all_to_all(rows.reshape(EXPERTS, n // EXPERTS, width), "dp", 0, 0).reshape(n, width)


def on_device(
    hidden_state_matrix,
    specialist_choice_ids,
    seat_quota_per_specialist,
    candidate_active_extent,
    normalizer_gain_vector,
    dispatcher_matrix,
    gating_matrices,
    expanding_matrices,
    contracting_matrices,
):
    tokens = hidden_state_matrix[0]
    ids = specialist_choice_ids[0].T
    gain = normalizer_gain_vector
    router = dispatcher_matrix[0]
    w_gate = gating_matrices[0, 0]
    w_up = expanding_matrices[0, 0]
    w_down = contracting_matrices[0, 0]
    n, width = tokens.shape
    slots = EXPERTS * SLOTS
    hid = w_gate.shape[0]
    half = (lax.axis_index("tensor") // 4).astype(jnp.int32)[None]

    table = jax.ShapeDtypeStruct((n, slots), BF)
    rows, match, held, chosen, which = call(
        route_body,
        (
            jax.ShapeDtypeStruct((n, width), BF),
            table,
            table,
            jax.ShapeDtypeStruct((n, EXPERTS), F32),
            jax.ShapeDtypeStruct((1,), jnp.int32),
        ),
        [VM] * 4,
        (ids, candidate_active_extent, seat_quota_per_specialist, tokens),
        out_specs=(VM, VM, VM, VM, SM),
        limit=16,
    )

    def first_part(size):
        def run(rows, held, gain, router):
            mine = rows[:size]
            far = along(mine, 4)
            return call(
                pick_first_body,
                (
                    jax.ShapeDtypeStruct((slots, 5 * width), BF),
                    jax.ShapeDtypeStruct((n, width), BF),
                    jax.ShapeDtypeStruct((n, 128), F32),
                    jax.ShapeDtypeStruct((n, EXPERTS), F32),
                ),
                [VM] * 5,
                (to_fours(mine), far, held, gain, router),
                limit=16,
            )

        return run

    def second_part(size):
        def run(far, held, gain, router, squares, logits, match, chosen):
            rest = [along(far[:size], by) for by in (1, 2, 3)]
            return call(
                pick_second_body,
                (jax.ShapeDtypeStruct((slots, 3 * width), BF), table, table),
                [VM] * 10,
                (*rest, held, gain, router, squares, logits, match, chosen),
                limit=16,
            )

        return run

    first, far, squares, logits = lax.switch(
        which[0], [first_part(size) for size in SIZES], rows, held, gain, router
    )
    first_rows = over_dp(first)
    second, high, low = lax.switch(
        which[0], [second_part(size) for size in SIZES], far, held, gain, router, squares, logits, match, chosen
    )
    first_rows, second = lax.optimization_barrier((first_rows, second))
    second_rows = over_dp(second)
    parts = jax.ShapeDtypeStruct((2 * hid + 8, slots), F32)
    weights = jax.ShapeDtypeStruct((3, hid, width), BF)
    parts, gate_rest, up_rest = call(
        expand_first_body,
        (parts, weights, weights),
        [VM] * 2 + [HB] * 2,
        (first_rows, gain, w_gate, w_up),
        [pltpu.VMEM((5, hid, width), BF)] * 2 + [pltpu.SemaphoreType.DMA((2, 8))],
        limit=16,
    )
    hidden = call(
        expand_second_body,
        jax.ShapeDtypeStruct((hid, slots), BF),
        [VM] * 5,
        (second_rows, parts, gain, gate_rest, up_rest),
        limit=16,
    )
    hidden_other = along(hidden, 4)
    hidden_first = to_fours(hidden)
    hidden_second = to_fours(hidden_other)
    reply = call(
        contract_body,
        jax.ShapeDtypeStruct((slots, width), BF),
        [SM] + [VM] * 3,
        (half, hidden_first, hidden_second, w_down),
    )
    returned = over_dp(reply)
    layer_out = call(
        mix_body, jax.ShapeDtypeStruct((n, width), BF), [VM] * 4, (high, low, returned, tokens)
    )
    count = lax.axis_size("section")
    handed = lax.ppermute(layer_out, "section", [(i, (i + 1) % count) for i in range(count)])
    return handed[None]


def solution(mesh):
    return jax.shard_map(
        on_device,
        mesh=mesh,
        in_specs=(
            P("section", "dp", "tensor"),
            P("section", "dp", None),
            P("section", None),
            P("section", "dp"),
            P("section", None),
            P("section", None, None),
            P("section", "dp", "tensor", None),
            P("section", "dp", "tensor", None),
            P("section", "dp", None, "tensor"),
        ),
        out_specs=P("section", "dp", "tensor"),
        check_vma=False,
    )
```

```python
import jax
import jax.numpy as jnp
from jax import lax
from jax.experimental import pallas as pl
from jax.experimental.pallas import tpu as pltpu
from jax.sharding import PartitionSpec as P

norm_eps = 1e-06
BF = jnp.bfloat16
F32 = jnp.float32
EXPERTS = 16
SLOTS = 16
VM = pl.BlockSpec(memory_space=pltpu.VMEM)
SM = pl.BlockSpec(memory_space=pltpu.SMEM)
HB = pl.BlockSpec(memory_space=pltpu.HBM)
SIZES = (48, 64, 80, 96, 128)
FOURS = [[0, 1, 2, 3], [4, 5, 6, 7]]


def dot(a, b, da, db):
    return lax.dot_general(a, b, (((da,), (db,)), ((), ())), preferred_element_type=F32)


def call(body, shape, specs, args, scratch=(), out_specs=None, flops=0, moved=0, limit=24):
    return pl.pallas_call(
        body,
        scratch_shapes=list(scratch),
        out_shape=shape,
        in_specs=specs,
        out_specs=out_specs or jax.tree.map(lambda _: VM, shape),
        compiler_params=pltpu.CompilerParams(vmem_limit_bytes=limit * 2**20),
        cost_estimate=pl.CostEstimate(flops=flops, bytes_accessed=moved, transcendentals=0),
    )(*args)


def eye(n):
    return (lax.broadcasted_iota(jnp.int32, (n, n), 0) == lax.broadcasted_iota(jnp.int32, (n, n), 1)).astype(BF)


def route_body(ids_ref, length_ref, quota_ref, tokens_ref, rows_ref, match_ref, held_ref, chosen_ref, which_ref):
    n = ids_ref.shape[1]
    expert = lax.broadcasted_iota(jnp.int32, (EXPERTS, n), 0)
    chosen = jnp.zeros((EXPERTS, n), F32)
    for j in range(ids_ref.shape[0]):
        chosen = chosen + (ids_ref[j : j + 1, :] == expert).astype(F32)
    at = lax.broadcasted_iota(jnp.int32, (1, n), 1)
    picked = chosen * (at < length_ref[...]).astype(F32)
    down = lax.broadcasted_iota(jnp.int32, (n, n), 0)
    before = (down < lax.broadcasted_iota(jnp.int32, (n, n), 1)).astype(BF)
    order = dot(picked.astype(BF), before, 1, 0)
    quota = jnp.sum(eye(EXPERTS).astype(F32) * quota_ref[...].astype(F32), axis=1, keepdims=True)
    kept = picked * (order < quota).astype(F32)
    slot = lax.broadcasted_iota(jnp.int32, (SLOTS, n), 0).astype(F32)
    hits = [(order[e : e + 1, :] == slot).astype(F32) * kept[e : e + 1, :] for e in range(EXPERTS)]
    match = dot(eye(n), jnp.concatenate(hits, axis=0).astype(BF), 1, 1).astype(BF)
    used = jnp.max(kept, axis=0, keepdims=True)
    place = dot(jnp.broadcast_to(used, (8, n)).astype(BF), before, 1, 0)[0:1, :]
    compact = ((place == down.astype(F32)).astype(F32) * used).astype(BF)
    rows_ref[...] = dot(compact, tokens_ref[...], 1, 0).astype(BF)
    match_ref[...] = match
    held_ref[...] = dot(compact, match, 1, 0).astype(BF)
    chosen_ref[...] = dot(compact, chosen.astype(BF), 1, 1)
    count = jnp.sum(used).astype(jnp.int32)
    which_ref[0] = sum((count > size).astype(jnp.int32) for size in SIZES[:-1])


def blocks_of(rank, width):
    order = [rank // 4 * 4 + k for k in range(4)] + [rank ^ 4 ^ k for k in range(4)]
    return [pl.ds(pl.multiple_of(r * width, width), width) for r in order]


def pick(views, blocks, held, gain_ref, router_ref, out_ref):
    n, width = views[0].shape
    squares = jnp.zeros((n, 1), F32)
    logits = jnp.zeros((n, EXPERTS), F32)
    for k, (view, cols) in enumerate(zip(views, blocks)):
        raw = view[...]
        out_ref[:, k * width : (k + 1) * width] = dot(held, raw, 0, 0).astype(BF)
        v = raw.astype(F32)
        squares = squares + jnp.sum(v * v, axis=1, keepdims=True)
        scaled = (v * gain_ref[:, cols].astype(F32)).astype(BF)
        logits = logits + dot(scaled, router_ref[:, cols], 1, 1)
    return squares, logits


def pick_first_body(own_ref, far_ref, held_ref, gain_ref, router_ref, out_ref, kept_far_ref, squares_ref, logits_ref):
    n, width = far_ref.shape
    blocks = blocks_of(lax.axis_index("tensor"), width)[:5]
    views = [own_ref.at[k] for k in range(4)] + [far_ref]
    squares, logits = pick(views, blocks, held_ref[0:n, :], gain_ref, router_ref, out_ref)
    kept_far_ref[0:n, :] = far_ref[...]
    squares_ref[0:n, :] = jnp.broadcast_to(squares, (n, squares_ref.shape[1]))
    logits_ref[0:n, :] = logits


def pick_second_body(
    a_ref, b_ref, c_ref, held_ref, gain_ref, router_ref, squares_ref, logits_ref, match_ref, chosen_ref,
    out_ref, high_ref, low_ref,
):
    n, width = a_ref.shape
    blocks = blocks_of(lax.axis_index("tensor"), width)[5:]
    held = held_ref[0:n, :]
    squares, logits = pick([a_ref, b_ref, c_ref], blocks, held, gain_ref, router_ref, out_ref)
    inverse = lax.rsqrt((squares + squares_ref[0:n, 0:1]) / (8 * width) + norm_eps)
    chosen = chosen_ref[0:n, :]
    powered = jnp.exp((logits + logits_ref[0:n, :]) * inverse) * chosen
    weight = powered / (jnp.sum(powered, axis=1, keepdims=True) + (1.0 - jnp.max(chosen, axis=1, keepdims=True)))
    slots = held.shape[1]
    owner = (
        lax.broadcasted_iota(jnp.int32, (EXPERTS, slots), 1) // SLOTS
        == lax.broadcasted_iota(jnp.int32, (EXPERTS, slots), 0)
    ).astype(BF)
    spread = jnp.zeros((n, slots), F32)
    for _ in range(3):
        piece = weight.astype(BF)
        spread = spread + dot(piece, owner, 1, 0)
        weight = weight - piece.astype(F32)
    row = jnp.sum(spread * held.astype(F32), axis=0, keepdims=True)
    value = match_ref[...].astype(F32) * row
    high = value.astype(BF)
    high_ref[...] = high
    low_ref[...] = (value - high.astype(F32)).astype(BF)


def partial_products(rows_ref, gain_ref, blocks, weights):
    rows = rows_ref.shape[0]
    squares = jnp.zeros((rows, 1), F32)
    gate = up = 0.0
    for k, cols in enumerate(blocks):
        width = rows_ref.shape[1] // len(blocks)
        v = rows_ref[:, k * width : (k + 1) * width].astype(F32)
        squares = squares + jnp.sum(v * v, axis=1, keepdims=True)
        scaled = (v * gain_ref[:, cols].astype(F32)).astype(BF)
        gate_part, up_part = weights(k)
        gate = gate + dot(gate_part, scaled, 1, 1)
        up = up + dot(up_part, scaled, 1, 1)
    return gate, up, jnp.broadcast_to(squares, (rows, 128)).T[0:1, :]


def expand_first_body(
    rows_ref, gain_ref, gate_ref, up_ref,
    parts_ref, gate_rest, up_rest, gate_buf, up_buf, sems,
):
    rank = lax.axis_index("tensor")
    now, _, width = gate_buf.shape
    blocks = blocks_of(rank, width)
    copies = []
    for k, cols in enumerate(blocks):
        targets = (gate_buf, up_buf) if k < now else (gate_rest, up_rest)
        at = k if k < now else k - now
        pair = [
            pltpu.make_async_copy(source.at[:, cols], target.at[at], sems.at[i, k])
            for i, (source, target) in enumerate(zip((gate_ref, up_ref), targets))
        ]
        for copy in pair:
            copy.start()
        copies.append(pair)

    def weights(k):
        for copy in copies[k]:
            copy.wait()
        return gate_buf[k], up_buf[k]

    gate, up, squares = partial_products(rows_ref, gain_ref, blocks[:now], weights)
    hid, rows = gate.shape
    parts_ref[0:hid, :] = gate
    parts_ref[hid : 2 * hid, :] = up
    parts_ref[2 * hid :, :] = jnp.broadcast_to(squares, (8, rows))
    for pair in copies[now:]:
        for copy in pair:
            copy.wait()


def expand_second_body(rows_ref, parts_ref, gain_ref, gate_rest, up_rest, out_ref):
    rank = lax.axis_index("tensor")
    parts, hid, width = gate_rest.shape
    blocks = blocks_of(rank, width)[8 - parts :]
    gate, up, squares = partial_products(
        rows_ref, gain_ref, blocks, lambda k: (gate_rest[k], up_rest[k])
    )
    inverse = lax.rsqrt((squares + parts_ref[2 * hid : 2 * hid + 1, :]) / (8 * width) + norm_eps)
    gate = (gate + parts_ref[0:hid, :]) * inverse
    up = (up + parts_ref[hid : 2 * hid, :]) * inverse
    out_ref[...] = (gate / (1.0 + jnp.exp(-gate)) * up).astype(BF)


def contract_body(first_ref, second_ref, down_ref, out_ref):
    parts, hid, _ = first_ref.shape
    side = lax.axis_index("tensor") // parts
    total = jnp.zeros(out_ref.shape, F32)
    for ref, half in ((first_ref, side), (second_ref, 1 - side)):
        for k in range(parts):
            rows = pl.ds(pl.multiple_of((half * parts + k) * hid, hid), hid)
            total = total + dot(ref[k], down_ref[rows, :], 0, 0)
    out_ref[...] = total.astype(BF)


def mix_body(high_ref, low_ref, reply_ref, tokens_ref, out_ref):
    mixed = dot(high_ref[...], reply_ref[...], 1, 0) + dot(low_ref[...], reply_ref[...], 1, 0)
    out_ref[...] = (tokens_ref[...].astype(F32) + mixed).astype(BF)


def to_fours(shard):
    copies = jnp.broadcast_to(shard[None], (4,) + shard.shape)
    return lax.all_to_all(copies, "tensor", 0, 0, axis_index_groups=FOURS)


def to_fours_apart(shard, always):
    same = jax.ShapeDtypeStruct((4,) + shard.shape, shard.dtype)
    return lax.cond(always, to_fours, lambda x: jnp.zeros(same.shape, same.dtype), shard)


def along(shard, by):
    return lax.ppermute(shard, "tensor", [(i, i ^ by) for i in range(8)])


def over_dp(rows):
    n, width = rows.shape
    return lax.all_to_all(rows.reshape(EXPERTS, n // EXPERTS, width), "dp", 0, 0).reshape(n, width)


def on_device(
    hidden_state_matrix,
    specialist_choice_ids,
    seat_quota_per_specialist,
    candidate_active_extent,
    normalizer_gain_vector,
    dispatcher_matrix,
    gating_matrices,
    expanding_matrices,
    contracting_matrices,
):
    tokens = hidden_state_matrix[0]
    ids = specialist_choice_ids[0].T
    gain = normalizer_gain_vector
    router = dispatcher_matrix[0]
    w_gate = gating_matrices[0, 0]
    w_up = expanding_matrices[0, 0]
    w_down = contracting_matrices[0, 0]
    n, width = tokens.shape
    slots = EXPERTS * SLOTS
    hid = w_gate.shape[0]

    table = jax.ShapeDtypeStruct((n, slots), BF)
    rows, match, held, chosen, which = call(
        route_body,
        (
            jax.ShapeDtypeStruct((n, width), BF),
            table,
            table,
            jax.ShapeDtypeStruct((n, EXPERTS), F32),
            jax.ShapeDtypeStruct((1,), jnp.int32),
        ),
        [VM] * 4,
        (ids, candidate_active_extent, seat_quota_per_specialist, tokens),
        out_specs=(VM, VM, VM, VM, SM),
        limit=16,
    )

    def first_part(size):
        def run(always, rows, held, gain, router):
            mine = rows[:size]
            far = along(mine, 4)
            return call(
                pick_first_body,
                (
                    jax.ShapeDtypeStruct((slots, 5 * width), BF),
                    jax.ShapeDtypeStruct((n, width), BF),
                    jax.ShapeDtypeStruct((n, 128), F32),
                    jax.ShapeDtypeStruct((n, EXPERTS), F32),
                ),
                [VM] * 5,
                (to_fours_apart(mine, always), far, held, gain, router),
                limit=16,
            )

        return run

    def second_part(size):
        def run(far, held, gain, router, squares, logits, match, chosen):
            rest = [along(far[:size], by) for by in (1, 2, 3)]
            return call(
                pick_second_body,
                (jax.ShapeDtypeStruct((slots, 3 * width), BF), table, table),
                [VM] * 10,
                (*rest, held, gain, router, squares, logits, match, chosen),
                limit=16,
            )

        return run

    always = which[0] < len(SIZES)
    first, far, squares, logits = lax.switch(
        which[0], [first_part(size) for size in SIZES], always, rows, held, gain, router
    )
    first_rows = over_dp(first)
    second, high, low = lax.switch(
        which[0], [second_part(size) for size in SIZES], far, held, gain, router, squares, logits, match, chosen
    )
    first_rows, second = lax.optimization_barrier((first_rows, second))
    second_rows = over_dp(second)
    parts = jax.ShapeDtypeStruct((2 * hid + 8, slots), F32)
    weights = jax.ShapeDtypeStruct((3, hid, width), BF)
    parts, gate_rest, up_rest = call(
        expand_first_body,
        (parts, weights, weights),
        [VM] * 2 + [HB] * 2,
        (first_rows, gain, w_gate, w_up),
        [pltpu.VMEM((5, hid, width), BF)] * 2 + [pltpu.SemaphoreType.DMA((2, 8))],
        limit=16,
    )
    hidden = call(
        expand_second_body,
        jax.ShapeDtypeStruct((hid, slots), BF),
        [VM] * 5,
        (second_rows, parts, gain, gate_rest, up_rest),
        limit=16,
    )
    hidden_other = along(hidden, 4)
    hidden_first = to_fours_apart(hidden, always)
    hidden_second = to_fours(hidden_other)
    reply = call(
        contract_body,
        jax.ShapeDtypeStruct((slots, width), BF),
        [VM] * 3,
        (hidden_first, hidden_second, w_down),
    )
    returned = over_dp(reply)
    layer_out = call(
        mix_body, jax.ShapeDtypeStruct((n, width), BF), [VM] * 4, (high, low, returned, tokens)
    )
    count = lax.axis_size("section")
    handed = lax.ppermute(layer_out, "section", [(i, (i + 1) % count) for i in range(count)])
    return handed[None]


def solution(mesh):
    return jax.shard_map(
        on_device,
        mesh=mesh,
        in_specs=(
            P("section", "dp", "tensor"),
            P("section", "dp", None),
            P("section", None),
            P("section", "dp"),
            P("section", None),
            P("section", None, None),
            P("section", "dp", "tensor", None),
            P("section", "dp", "tensor", None),
            P("section", "dp", None, "tensor"),
        ),
        out_specs=P("section", "dp", "tensor"),
        check_vma=False,
    )
```

```python
import jax
import jax.numpy as jnp
from jax import lax
from jax.experimental import pallas as pl
from jax.experimental.pallas import tpu as pltpu
from jax.sharding import PartitionSpec as P

norm_eps = 1e-06
BF = jnp.bfloat16
F32 = jnp.float32
EXPERTS = 16
SLOTS = 16
VM = pl.BlockSpec(memory_space=pltpu.VMEM)
SM = pl.BlockSpec(memory_space=pltpu.SMEM)
HB = pl.BlockSpec(memory_space=pltpu.HBM)
SIZES = (48, 64, 80, 96, 128)
FOURS = [[0, 1, 2, 3], [4, 5, 6, 7]]


def dot(a, b, da, db):
    return lax.dot_general(a, b, (((da,), (db,)), ((), ())), preferred_element_type=F32)


def call(body, shape, specs, args, scratch=(), out_specs=None, flops=0, moved=0, limit=24):
    return pl.pallas_call(
        body,
        scratch_shapes=list(scratch),
        out_shape=shape,
        in_specs=specs,
        out_specs=out_specs or jax.tree.map(lambda _: VM, shape),
        compiler_params=pltpu.CompilerParams(vmem_limit_bytes=limit * 2**20),
        cost_estimate=pl.CostEstimate(flops=flops, bytes_accessed=moved, transcendentals=0),
    )(*args)


def eye(n):
    return (lax.broadcasted_iota(jnp.int32, (n, n), 0) == lax.broadcasted_iota(jnp.int32, (n, n), 1)).astype(BF)


def route_body(ids_ref, length_ref, quota_ref, tokens_ref, rows_ref, again_ref, match_ref, held_ref, chosen_ref, which_ref):
    n = ids_ref.shape[1]
    expert = lax.broadcasted_iota(jnp.int32, (EXPERTS, n), 0)
    chosen = jnp.zeros((EXPERTS, n), F32)
    for j in range(ids_ref.shape[0]):
        chosen = chosen + (ids_ref[j : j + 1, :] == expert).astype(F32)
    at = lax.broadcasted_iota(jnp.int32, (1, n), 1)
    picked = chosen * (at < length_ref[...]).astype(F32)
    down = lax.broadcasted_iota(jnp.int32, (n, n), 0)
    before = (down < lax.broadcasted_iota(jnp.int32, (n, n), 1)).astype(BF)
    order = dot(picked.astype(BF), before, 1, 0)
    quota = jnp.sum(eye(EXPERTS).astype(F32) * quota_ref[...].astype(F32), axis=1, keepdims=True)
    kept = picked * (order < quota).astype(F32)
    slot = lax.broadcasted_iota(jnp.int32, (SLOTS, n), 0).astype(F32)
    hits = [(order[e : e + 1, :] == slot).astype(F32) * kept[e : e + 1, :] for e in range(EXPERTS)]
    match = dot(eye(n), jnp.concatenate(hits, axis=0).astype(BF), 1, 1).astype(BF)
    used = jnp.max(kept, axis=0, keepdims=True)
    place = dot(jnp.broadcast_to(used, (8, n)).astype(BF), before, 1, 0)[0:1, :]
    compact = ((place == down.astype(F32)).astype(F32) * used).astype(BF)
    rows = dot(compact, tokens_ref[...], 1, 0).astype(BF)
    rows_ref[...] = rows
    again_ref[...] = rows
    match_ref[...] = match
    held_ref[...] = dot(compact, match, 1, 0).astype(BF)
    chosen_ref[...] = dot(compact, chosen.astype(BF), 1, 1)
    count = jnp.sum(used).astype(jnp.int32)
    which_ref[0] = sum((count > size).astype(jnp.int32) for size in SIZES[:-1])


def blocks_of(rank, width):
    order = [rank // 4 * 4 + k for k in range(4)] + [rank ^ 4 ^ k for k in range(4)]
    return [pl.ds(pl.multiple_of(r * width, width), width) for r in order]


def pick(views, blocks, held, gain_ref, router_ref, out_ref, leave):
    n, width = views[0].shape
    squares = jnp.zeros((n, 1), F32)
    logits = jnp.zeros((n, EXPERTS), F32)
    for k, (view, cols) in enumerate(zip(views, blocks)):
        raw = view[...]
        out_ref[k] = dot(held, raw, 0, 0).astype(BF)
        leave(k)
        v = raw.astype(F32)
        squares = squares + jnp.sum(v * v, axis=1, keepdims=True)
        scaled = (v * gain_ref[:, cols].astype(F32)).astype(BF)
        logits = logits + dot(scaled, router_ref[:, cols], 1, 1)
    return squares, logits


def pick_first_body(own_ref, far_ref, held_ref, gain_ref, router_ref, out_ref, kept_far_ref, squares_ref, logits_ref, buffer, sems):
    n, width = far_ref.shape
    blocks = blocks_of(lax.axis_index("tensor"), width)[:5]
    views = [own_ref.at[k] for k in range(4)] + [far_ref]
    copies = []

    def leave(k):
        cols = slice(k * width, (k + 1) * width)
        copies.append(pltpu.make_async_copy(buffer.at[k], out_ref.at[:, cols], sems.at[k]))
        copies[k].start()

    squares, logits = pick(views, blocks, held_ref[0:n, :], gain_ref, router_ref, buffer, leave)
    kept_far_ref[0:n, :] = far_ref[...]
    squares_ref[0:n, :] = jnp.broadcast_to(squares, (n, squares_ref.shape[1]))
    logits_ref[0:n, :] = logits
    for copy in copies:
        copy.wait()


def pick_second_body(
    a_ref, b_ref, c_ref, held_ref, gain_ref, router_ref, squares_ref, logits_ref, match_ref, chosen_ref,
    out_ref, high_ref, low_ref, buffer, sems,
):
    n, width = a_ref.shape
    blocks = blocks_of(lax.axis_index("tensor"), width)[5:]
    held = held_ref[0:n, :]
    copies = []

    def leave(k):
        cols = slice(k * width, (k + 1) * width)
        copies.append(pltpu.make_async_copy(buffer.at[k], out_ref.at[:, cols], sems.at[k]))
        copies[k].start()

    squares, logits = pick([a_ref, b_ref, c_ref], blocks, held, gain_ref, router_ref, buffer, leave)
    inverse = lax.rsqrt((squares + squares_ref[0:n, 0:1]) / (8 * width) + norm_eps)
    chosen = chosen_ref[0:n, :]
    powered = jnp.exp((logits + logits_ref[0:n, :]) * inverse) * chosen
    weight = powered / (jnp.sum(powered, axis=1, keepdims=True) + (1.0 - jnp.max(chosen, axis=1, keepdims=True)))
    slots = held.shape[1]
    owner = (
        lax.broadcasted_iota(jnp.int32, (EXPERTS, slots), 1) // SLOTS
        == lax.broadcasted_iota(jnp.int32, (EXPERTS, slots), 0)
    ).astype(BF)
    spread = jnp.zeros((n, slots), F32)
    for _ in range(3):
        piece = weight.astype(BF)
        spread = spread + dot(piece, owner, 1, 0)
        weight = weight - piece.astype(F32)
    row = jnp.sum(spread * held.astype(F32), axis=0, keepdims=True)
    value = match_ref[...].astype(F32) * row
    high = value.astype(BF)
    high_ref[...] = high
    low_ref[...] = (value - high.astype(F32)).astype(BF)
    for copy in copies:
        copy.wait()


def partial_products(rows_ref, gain_ref, blocks, weights):
    rows = rows_ref.shape[0]
    squares = jnp.zeros((rows, 1), F32)
    gate = up = 0.0
    for k, cols in enumerate(blocks):
        width = rows_ref.shape[1] // len(blocks)
        v = rows_ref[:, k * width : (k + 1) * width].astype(F32)
        squares = squares + jnp.sum(v * v, axis=1, keepdims=True)
        scaled = (v * gain_ref[:, cols].astype(F32)).astype(BF)
        gate_part, up_part = weights(k)
        gate = gate + dot(gate_part, scaled, 1, 1)
        up = up + dot(up_part, scaled, 1, 1)
    return gate, up, jnp.broadcast_to(squares, (rows, 128)).T[0:1, :]


def expand_first_body(
    rows_ref, gain_ref, gate_ref, up_ref,
    parts_ref, gate_rest, up_rest, gate_buf, up_buf, sems,
):
    rank = lax.axis_index("tensor")
    now, _, width = gate_buf.shape
    blocks = blocks_of(rank, width)
    copies = []
    for k, cols in enumerate(blocks):
        targets = (gate_buf, up_buf) if k < now else (gate_rest, up_rest)
        at = k if k < now else k - now
        pair = [
            pltpu.make_async_copy(source.at[:, cols], target.at[at], sems.at[i, k])
            for i, (source, target) in enumerate(zip((gate_ref, up_ref), targets))
        ]
        for copy in pair:
            copy.start()
        copies.append(pair)

    def weights(k):
        for copy in copies[k]:
            copy.wait()
        return gate_buf[k], up_buf[k]

    gate, up, squares = partial_products(rows_ref, gain_ref, blocks[:now], weights)
    hid, rows = gate.shape
    parts_ref[0:hid, :] = gate
    parts_ref[hid : 2 * hid, :] = up
    parts_ref[2 * hid :, :] = jnp.broadcast_to(squares, (8, rows))
    for pair in copies[now:]:
        for copy in pair:
            copy.wait()


def expand_second_body(rows_ref, parts_hbm, gain_ref, gate_rest, up_rest, out_ref, copies_ref, parts_ref, sem):
    rank = lax.axis_index("tensor")
    parts, hid, width = gate_rest.shape
    copy = pltpu.make_async_copy(parts_hbm, parts_ref, sem)
    copy.start()
    blocks = blocks_of(rank, width)[8 - parts :]
    gate, up, squares = partial_products(
        rows_ref, gain_ref, blocks, lambda k: (gate_rest[k], up_rest[k])
    )
    copy.wait()
    inverse = lax.rsqrt((squares + parts_ref[2 * hid : 2 * hid + 1, :]) / (8 * width) + norm_eps)
    gate = (gate + parts_ref[0:hid, :]) * inverse
    up = (up + parts_ref[hid : 2 * hid, :]) * inverse
    hidden = (gate / (1.0 + jnp.exp(-gate)) * up).astype(BF)
    out_ref[...] = hidden
    for k in range(4):
        copies_ref[k] = hidden


def contract_body(first_ref, second_ref, down_ref, out_ref):
    parts, hid, _ = first_ref.shape
    side = lax.axis_index("tensor") // parts
    total = jnp.zeros(out_ref.shape, F32)
    for ref, half in ((first_ref, side), (second_ref, 1 - side)):
        for k in range(parts):
            rows = pl.ds(pl.multiple_of((half * parts + k) * hid, hid), hid)
            total = total + dot(ref[k], down_ref[rows, :], 0, 0)
    out_ref[...] = total.astype(BF)


def mix_body(high_ref, low_ref, reply_ref, tokens_ref, out_ref):
    mixed = dot(high_ref[...], reply_ref[...], 1, 0) + dot(low_ref[...], reply_ref[...], 1, 0)
    out_ref[...] = (tokens_ref[...].astype(F32) + mixed).astype(BF)


def fours(copies):
    return lax.all_to_all(copies, "tensor", 0, 0, axis_index_groups=FOURS)


def to_fours(shard):
    return fours(jnp.broadcast_to(shard[None], (4,) + shard.shape))


def to_fours_apart(rows, size, always):
    shape = (4, size) + rows.shape[1:]
    return lax.cond(always, lambda x: to_fours(x[:size]), lambda x: jnp.zeros(shape, x.dtype), rows)


def along(shard, by):
    return lax.ppermute(shard, "tensor", [(i, i ^ by) for i in range(8)])


def over_dp(rows):
    n, width = rows.shape
    return lax.all_to_all(rows.reshape(EXPERTS, n // EXPERTS, width), "dp", 0, 0).reshape(n, width)


def on_device(
    hidden_state_matrix,
    specialist_choice_ids,
    seat_quota_per_specialist,
    candidate_active_extent,
    normalizer_gain_vector,
    dispatcher_matrix,
    gating_matrices,
    expanding_matrices,
    contracting_matrices,
):
    tokens = hidden_state_matrix[0]
    ids = specialist_choice_ids[0].T
    gain = normalizer_gain_vector
    router = dispatcher_matrix[0]
    w_gate = gating_matrices[0, 0]
    w_up = expanding_matrices[0, 0]
    w_down = contracting_matrices[0, 0]
    n, width = tokens.shape
    slots = EXPERTS * SLOTS
    hid = w_gate.shape[0]

    table = jax.ShapeDtypeStruct((n, slots), BF)
    rows, again, match, held, chosen, which = call(
        route_body,
        (
            jax.ShapeDtypeStruct((n, width), BF),
            jax.ShapeDtypeStruct((n, width), BF),
            table,
            table,
            jax.ShapeDtypeStruct((n, EXPERTS), F32),
            jax.ShapeDtypeStruct((1,), jnp.int32),
        ),
        [VM] * 4,
        (ids, candidate_active_extent, seat_quota_per_specialist, tokens),
        out_specs=(VM,) * 5 + (SM,),
        limit=16,
    )

    def first_part(size):
        def run(which, rows, again, held, gain, router):
            far = along(rows[:size], 4)
            return call(
                pick_first_body,
                (
                    jax.ShapeDtypeStruct((slots, 5 * width), BF),
                    jax.ShapeDtypeStruct((n, width), BF),
                    jax.ShapeDtypeStruct((n, 128), F32),
                    jax.ShapeDtypeStruct((n, EXPERTS), F32),
                ),
                [VM] * 5,
                (to_fours_apart(again, size, which[0] < len(SIZES)), far, held, gain, router),
                [pltpu.VMEM((5, slots, width), BF), pltpu.SemaphoreType.DMA((5,))],
                out_specs=(HB, VM, VM, VM),
                limit=16,
            )

        return run

    def second_part(size):
        def run(far, held, gain, router, squares, logits, match, chosen):
            rest = [along(far[:size], by) for by in (1, 2, 3)]
            return call(
                pick_second_body,
                (jax.ShapeDtypeStruct((slots, 3 * width), BF), table, table),
                [VM] * 10,
                (*rest, held, gain, router, squares, logits, match, chosen),
                [pltpu.VMEM((3, slots, width), BF), pltpu.SemaphoreType.DMA((3,))],
                out_specs=(HB, VM, VM),
                limit=16,
            )

        return run

    always = which[0] < len(SIZES)
    first, far, squares, logits = lax.switch(
        which[0], [first_part(size) for size in SIZES], which, rows, again, held, gain, router
    )
    first_rows = over_dp(first)
    second, high, low = lax.switch(
        which[0], [second_part(size) for size in SIZES], far, held, gain, router, squares, logits, match, chosen
    )
    first_rows, second = lax.optimization_barrier((first_rows, second))
    second_rows = over_dp(second)
    parts = jax.ShapeDtypeStruct((2 * hid + 8, slots), F32)
    weights = jax.ShapeDtypeStruct((3, hid, width), BF)
    parts, gate_rest, up_rest = call(
        expand_first_body,
        (parts, weights, weights),
        [VM] * 2 + [HB] * 2,
        (first_rows, gain, w_gate, w_up),
        [pltpu.VMEM((5, hid, width), BF)] * 2 + [pltpu.SemaphoreType.DMA((2, 8))],
        limit=16,
    )
    hidden, copies = call(
        expand_second_body,
        (jax.ShapeDtypeStruct((hid, slots), BF), jax.ShapeDtypeStruct((4, hid, slots), BF)),
        [VM, HB, VM, VM, VM],
        (second_rows, parts, gain, gate_rest, up_rest),
        [pltpu.VMEM((2 * hid + 8, slots), F32), pltpu.SemaphoreType.DMA],
        limit=16,
    )
    hidden_other = along(hidden, 4)
    hidden_first = lax.cond(always, fours, jnp.zeros_like, copies)
    hidden_second = to_fours(hidden_other)
    reply = call(
        contract_body,
        jax.ShapeDtypeStruct((slots, width), BF),
        [VM] * 3,
        (hidden_first, hidden_second, w_down),
    )
    returned = over_dp(reply)
    layer_out = call(
        mix_body, jax.ShapeDtypeStruct((n, width), BF), [VM] * 4, (high, low, returned, tokens)
    )
    count = lax.axis_size("section")
    handed = lax.ppermute(layer_out, "section", [(i, (i + 1) % count) for i in range(count)])
    return handed[None]


def solution(mesh):
    return jax.shard_map(
        on_device,
        mesh=mesh,
        in_specs=(
            P("section", "dp", "tensor"),
            P("section", "dp", None),
            P("section", None),
            P("section", "dp"),
            P("section", None),
            P("section", None, None),
            P("section", "dp", "tensor", None),
            P("section", "dp", "tensor", None),
            P("section", "dp", None, "tensor"),
        ),
        out_specs=P("section", "dp", "tensor"),
        check_vma=False,
    )
```

```python
import jax
import jax.numpy as jnp
from jax import lax
from jax.experimental import pallas as pl
from jax.experimental.pallas import tpu as pltpu
from jax.sharding import PartitionSpec as P

norm_eps = 1e-06
BF = jnp.bfloat16
F32 = jnp.float32
EXPERTS = 16
SLOTS = 16
VM = pl.BlockSpec(memory_space=pltpu.VMEM)
SM = pl.BlockSpec(memory_space=pltpu.SMEM)
HB = pl.BlockSpec(memory_space=pltpu.HBM)
SIZES = (48, 64, 80, 96, 128)
FOURS = [[0, 1, 2, 3], [4, 5, 6, 7]]


def dot(a, b, da, db):
    return lax.dot_general(a, b, (((da,), (db,)), ((), ())), preferred_element_type=F32)


def call(body, shape, specs, args, scratch=(), out_specs=None, flops=0, moved=0, limit=24):
    return pl.pallas_call(
        body,
        scratch_shapes=list(scratch),
        out_shape=shape,
        in_specs=specs,
        out_specs=out_specs or jax.tree.map(lambda _: VM, shape),
        compiler_params=pltpu.CompilerParams(vmem_limit_bytes=limit * 2**20),
        cost_estimate=pl.CostEstimate(flops=flops, bytes_accessed=moved, transcendentals=0),
    )(*args)


def eye(n):
    return (lax.broadcasted_iota(jnp.int32, (n, n), 0) == lax.broadcasted_iota(jnp.int32, (n, n), 1)).astype(BF)


def route_body(ids_ref, length_ref, quota_ref, tokens_ref, rows_ref, again_ref, match_ref, held_ref, chosen_ref, which_ref):
    n = ids_ref.shape[1]
    expert = lax.broadcasted_iota(jnp.int32, (EXPERTS, n), 0)
    chosen = jnp.zeros((EXPERTS, n), F32)
    for j in range(ids_ref.shape[0]):
        chosen = chosen + (ids_ref[j : j + 1, :] == expert).astype(F32)
    at = lax.broadcasted_iota(jnp.int32, (1, n), 1)
    picked = chosen * (at < length_ref[...]).astype(F32)
    down = lax.broadcasted_iota(jnp.int32, (n, n), 0)
    before = (down < lax.broadcasted_iota(jnp.int32, (n, n), 1)).astype(BF)
    order = dot(picked.astype(BF), before, 1, 0)
    quota = jnp.sum(eye(EXPERTS).astype(F32) * quota_ref[...].astype(F32), axis=1, keepdims=True)
    kept = picked * (order < quota).astype(F32)
    slot = lax.broadcasted_iota(jnp.int32, (SLOTS, n), 0).astype(F32)
    hits = [(order[e : e + 1, :] == slot).astype(F32) * kept[e : e + 1, :] for e in range(EXPERTS)]
    match = dot(eye(n), jnp.concatenate(hits, axis=0).astype(BF), 1, 1).astype(BF)
    used = jnp.max(kept, axis=0, keepdims=True)
    place = dot(jnp.broadcast_to(used, (8, n)).astype(BF), before, 1, 0)[0:1, :]
    compact = ((place == down.astype(F32)).astype(F32) * used).astype(BF)
    rows = dot(compact, tokens_ref[...], 1, 0).astype(BF)
    rows_ref[...] = rows
    again_ref[...] = rows
    match_ref[...] = match
    held_ref[...] = dot(compact, match, 1, 0).astype(BF)
    chosen_ref[...] = dot(compact, chosen.astype(BF), 1, 1)
    count = jnp.sum(used).astype(jnp.int32)
    which_ref[0] = sum((count > size).astype(jnp.int32) for size in SIZES[:-1])


def blocks_of(rank, width):
    order = [rank // 4 * 4 + k for k in range(4)] + [rank ^ 4 ^ k for k in range(4)]
    return [pl.ds(pl.multiple_of(r * width, width), width) for r in order]


def pick(views, blocks, held, gain_ref, router_ref, out_ref, leave):
    n, width = views[0].shape
    squares = jnp.zeros((n, 1), F32)
    logits = jnp.zeros((n, EXPERTS), F32)
    for k, (view, cols) in enumerate(zip(views, blocks)):
        raw = view[...]
        out_ref[k] = dot(held, raw, 0, 0).astype(BF)
        leave(k)
        v = raw.astype(F32)
        squares = squares + jnp.sum(v * v, axis=1, keepdims=True)
        scaled = (v * gain_ref[:, cols].astype(F32)).astype(BF)
        logits = logits + dot(scaled, router_ref[:, cols], 1, 1)
    return squares, logits


def pick_first_body(own_ref, far_ref, held_ref, gain_ref, router_ref, out_ref, kept_far_ref, squares_ref, logits_ref, buffer, sems):
    n, width = far_ref.shape
    blocks = blocks_of(lax.axis_index("tensor"), width)[:5]
    views = [own_ref.at[k] for k in range(4)] + [far_ref]
    copies = []

    def leave(k):
        cols = slice(k * width, (k + 1) * width)
        copies.append(pltpu.make_async_copy(buffer.at[k], out_ref.at[:, cols], sems.at[k]))
        copies[k].start()

    squares, logits = pick(views, blocks, held_ref[0:n, :], gain_ref, router_ref, buffer, leave)
    kept_far_ref[0:n, :] = far_ref[...]
    squares_ref[0:n, :] = jnp.broadcast_to(squares, (n, squares_ref.shape[1]))
    logits_ref[0:n, :] = logits
    for copy in copies:
        copy.wait()


def pick_second_body(
    a_ref, b_ref, c_ref, held_ref, gain_ref, router_ref, squares_ref, logits_ref, match_ref, chosen_ref,
    out_ref, high_ref, low_ref, buffer, sems,
):
    n, width = a_ref.shape
    blocks = blocks_of(lax.axis_index("tensor"), width)[5:]
    held = held_ref[0:n, :]
    copies = []

    def leave(k):
        cols = slice(k * width, (k + 1) * width)
        copies.append(pltpu.make_async_copy(buffer.at[k], out_ref.at[:, cols], sems.at[k]))
        copies[k].start()

    squares, logits = pick([a_ref, b_ref, c_ref], blocks, held, gain_ref, router_ref, buffer, leave)
    inverse = lax.rsqrt((squares + squares_ref[0:n, 0:1]) / (8 * width) + norm_eps)
    chosen = chosen_ref[0:n, :]
    powered = jnp.exp((logits + logits_ref[0:n, :]) * inverse) * chosen
    weight = powered / (jnp.sum(powered, axis=1, keepdims=True) + (1.0 - jnp.max(chosen, axis=1, keepdims=True)))
    slots = held.shape[1]
    owner = (
        lax.broadcasted_iota(jnp.int32, (EXPERTS, slots), 1) // SLOTS
        == lax.broadcasted_iota(jnp.int32, (EXPERTS, slots), 0)
    ).astype(BF)
    spread = jnp.zeros((n, slots), F32)
    for _ in range(3):
        piece = weight.astype(BF)
        spread = spread + dot(piece, owner, 1, 0)
        weight = weight - piece.astype(F32)
    row = jnp.sum(spread * held.astype(F32), axis=0, keepdims=True)
    value = match_ref[...].astype(F32) * row
    high = value.astype(BF)
    high_ref[...] = high
    low_ref[...] = (value - high.astype(F32)).astype(BF)
    for copy in copies:
        copy.wait()


def partial_products(rows_ref, gain_ref, blocks, weights):
    rows = rows_ref.shape[0]
    squares = jnp.zeros((rows, 1), F32)
    gate = up = 0.0
    for k, cols in enumerate(blocks):
        width = rows_ref.shape[1] // len(blocks)
        v = rows_ref[:, k * width : (k + 1) * width].astype(F32)
        squares = squares + jnp.sum(v * v, axis=1, keepdims=True)
        scaled = (v * gain_ref[:, cols].astype(F32)).astype(BF)
        gate_part, up_part = weights(k)
        gate = gate + dot(gate_part, scaled, 1, 1)
        up = up + dot(up_part, scaled, 1, 1)
    return gate, up, jnp.broadcast_to(squares, (rows, 128)).T[0:1, :]


def expand_first_body(
    rows_ref, gain_ref, gate_ref, up_ref,
    parts_ref, gate_rest, up_rest, gate_buf, up_buf, sems,
):
    rank = lax.axis_index("tensor")
    now, _, width = gate_buf.shape
    blocks = blocks_of(rank, width)
    copies = []
    for k, cols in enumerate(blocks):
        targets = (gate_buf, up_buf) if k < now else (gate_rest, up_rest)
        at = k if k < now else k - now
        pair = [
            pltpu.make_async_copy(source.at[:, cols], target.at[at], sems.at[i, k])
            for i, (source, target) in enumerate(zip((gate_ref, up_ref), targets))
        ]
        for copy in pair:
            copy.start()
        copies.append(pair)

    def weights(k):
        for copy in copies[k]:
            copy.wait()
        return gate_buf[k], up_buf[k]

    gate, up, squares = partial_products(rows_ref, gain_ref, blocks[:now], weights)
    hid, rows = gate.shape
    parts_ref[0:hid, :] = gate
    parts_ref[hid : 2 * hid, :] = up
    parts_ref[2 * hid :, :] = jnp.broadcast_to(squares, (8, rows))
    for pair in copies[now:]:
        for copy in pair:
            copy.wait()


def expand_second_body(rows_ref, parts_hbm, gain_ref, gate_rest, up_rest, out_ref, copies_ref, parts_ref, sem):
    rank = lax.axis_index("tensor")
    parts, hid, width = gate_rest.shape
    copy = pltpu.make_async_copy(parts_hbm, parts_ref, sem)
    copy.start()
    blocks = blocks_of(rank, width)[8 - parts :]
    gate, up, squares = partial_products(
        rows_ref, gain_ref, blocks, lambda k: (gate_rest[k], up_rest[k])
    )
    copy.wait()
    inverse = lax.rsqrt((squares + parts_ref[2 * hid : 2 * hid + 1, :]) / (8 * width) + norm_eps)
    gate = (gate + parts_ref[0:hid, :]) * inverse
    up = (up + parts_ref[hid : 2 * hid, :]) * inverse
    hidden = (gate / (1.0 + jnp.exp(-gate)) * up).astype(BF)
    out_ref[...] = hidden
    for k in range(4):
        copies_ref[k] = hidden


def contract_body(first_ref, second_ref, down_ref, out_ref):
    parts, hid, _ = first_ref.shape
    side = lax.axis_index("tensor") // parts
    total = jnp.zeros(out_ref.shape, F32)
    for ref, half in ((first_ref, side), (second_ref, 1 - side)):
        for k in range(parts):
            rows = pl.ds(pl.multiple_of((half * parts + k) * hid, hid), hid)
            total = total + dot(ref[k], down_ref[rows, :], 0, 0)
    out_ref[...] = total.astype(BF)


def mix_body(high_ref, low_ref, reply_ref, tokens_ref, out_ref):
    mixed = dot(high_ref[...], reply_ref[...], 1, 0) + dot(low_ref[...], reply_ref[...], 1, 0)
    out_ref[...] = (tokens_ref[...].astype(F32) + mixed).astype(BF)


def fours(copies):
    return lax.all_to_all(copies, "tensor", 0, 0, axis_index_groups=FOURS)


def to_fours(shard):
    return fours(jnp.broadcast_to(shard[None], (4,) + shard.shape))


def to_fours_apart(rows, size, always):
    shape = (4, size) + rows.shape[1:]
    return lax.cond(always, lambda x: to_fours(x[:size]), lambda x: jnp.zeros(shape, x.dtype), rows)


def along(shard, by):
    return lax.ppermute(shard, "tensor", [(i, i ^ by) for i in range(8)])


def over_dp(rows):
    n, width = rows.shape
    return lax.all_to_all(rows.reshape(EXPERTS, n // EXPERTS, width), "dp", 0, 0).reshape(n, width)


def on_device(
    hidden_state_matrix,
    specialist_choice_ids,
    seat_quota_per_specialist,
    candidate_active_extent,
    normalizer_gain_vector,
    dispatcher_matrix,
    gating_matrices,
    expanding_matrices,
    contracting_matrices,
):
    tokens = hidden_state_matrix[0]
    ids = specialist_choice_ids[0].T
    gain = normalizer_gain_vector
    router = dispatcher_matrix[0]
    w_gate = gating_matrices[0, 0]
    w_up = expanding_matrices[0, 0]
    w_down = contracting_matrices[0, 0]
    n, width = tokens.shape
    slots = EXPERTS * SLOTS
    hid = w_gate.shape[0]

    table = jax.ShapeDtypeStruct((n, slots), BF)
    rows, again, match, held, chosen, which = call(
        route_body,
        (
            jax.ShapeDtypeStruct((n, width), BF),
            jax.ShapeDtypeStruct((n, width), BF),
            table,
            table,
            jax.ShapeDtypeStruct((n, EXPERTS), F32),
            jax.ShapeDtypeStruct((1,), jnp.int32),
        ),
        [VM] * 4,
        (ids, candidate_active_extent, seat_quota_per_specialist, tokens),
        out_specs=(VM,) * 5 + (SM,),
        limit=16,
    )

    def first_part(size):
        def run(which, rows, again, held, gain, router):
            far = along(rows[:size], 4)
            return call(
                pick_first_body,
                (
                    jax.ShapeDtypeStruct((slots, 5 * width), BF),
                    jax.ShapeDtypeStruct((n, width), BF),
                    jax.ShapeDtypeStruct((n, 128), F32),
                    jax.ShapeDtypeStruct((n, EXPERTS), F32),
                ),
                [VM] * 5,
                (to_fours_apart(again, size, which[0] < len(SIZES)), far, held, gain, router),
                [pltpu.VMEM((5, slots, width), BF), pltpu.SemaphoreType.DMA((5,))],
                out_specs=(HB, VM, VM, VM),
                limit=16,
            )

        return run

    def second_part(size):
        def run(far, held, gain, router, squares, logits, match, chosen):
            rest = [along(far[:size], by) for by in (1, 2, 3)]
            return call(
                pick_second_body,
                (jax.ShapeDtypeStruct((slots, 3 * width), BF), table, table),
                [VM] * 10,
                (*rest, held, gain, router, squares, logits, match, chosen),
                [pltpu.VMEM((3, slots, width), BF), pltpu.SemaphoreType.DMA((3,))],
                out_specs=(HB, VM, VM),
                limit=16,
            )

        return run

    first, far, squares, logits = lax.switch(
        which[0], [first_part(size) for size in SIZES], which, rows, again, held, gain, router
    )
    first_rows = over_dp(first)
    second, high, low = lax.switch(
        which[0], [second_part(size) for size in SIZES], far, held, gain, router, squares, logits, match, chosen
    )
    first_rows, second = lax.optimization_barrier((first_rows, second))
    second_rows = over_dp(second)
    parts = jax.ShapeDtypeStruct((2 * hid + 8, slots), F32)
    weights = jax.ShapeDtypeStruct((3, hid, width), BF)
    parts, gate_rest, up_rest = call(
        expand_first_body,
        (parts, weights, weights),
        [VM] * 2 + [HB] * 2,
        (first_rows, gain, w_gate, w_up),
        [pltpu.VMEM((5, hid, width), BF)] * 2 + [pltpu.SemaphoreType.DMA((2, 8))],
        limit=16,
    )
    hidden, copies = call(
        expand_second_body,
        (jax.ShapeDtypeStruct((hid, slots), BF), jax.ShapeDtypeStruct((4, hid, slots), BF)),
        [VM, HB, VM, VM, VM],
        (second_rows, parts, gain, gate_rest, up_rest),
        [pltpu.VMEM((2 * hid + 8, slots), F32), pltpu.SemaphoreType.DMA],
        limit=16,
    )
    hidden_other = along(hidden, 4)
    hidden_first = fours(copies)
    hidden_second = to_fours(hidden_other)
    reply = call(
        contract_body,
        jax.ShapeDtypeStruct((slots, width), BF),
        [VM] * 3,
        (hidden_first, hidden_second, w_down),
    )
    returned = over_dp(reply)
    layer_out = call(
        mix_body, jax.ShapeDtypeStruct((n, width), BF), [VM] * 4, (high, low, returned, tokens)
    )
    count = lax.axis_size("section")
    handed = lax.ppermute(layer_out, "section", [(i, (i + 1) % count) for i in range(count)])
    return handed[None]


def solution(mesh):
    return jax.shard_map(
        on_device,
        mesh=mesh,
        in_specs=(
            P("section", "dp", "tensor"),
            P("section", "dp", None),
            P("section", None),
            P("section", "dp"),
            P("section", None),
            P("section", None, None),
            P("section", "dp", "tensor", None),
            P("section", "dp", "tensor", None),
            P("section", "dp", None, "tensor"),
        ),
        out_specs=P("section", "dp", "tensor"),
        check_vma=False,
    )
```

```python
import jax
import jax.numpy as jnp
from jax import lax
from jax.experimental import pallas as pl
from jax.experimental.pallas import tpu as pltpu
from jax.sharding import PartitionSpec as P

norm_eps = 1e-06
BF = jnp.bfloat16
F32 = jnp.float32
EXPERTS = 16
SLOTS = 16
VM = pl.BlockSpec(memory_space=pltpu.VMEM)
SM = pl.BlockSpec(memory_space=pltpu.SMEM)
HB = pl.BlockSpec(memory_space=pltpu.HBM)
SIZES = (48, 64, 80, 96, 128)
FOURS = [[0, 1, 2, 3], [4, 5, 6, 7]]


def dot(a, b, da, db):
    return lax.dot_general(a, b, (((da,), (db,)), ((), ())), preferred_element_type=F32)


def call(body, shape, specs, args, scratch=(), out_specs=None, flops=0, moved=0, limit=24):
    return pl.pallas_call(
        body,
        scratch_shapes=list(scratch),
        out_shape=shape,
        in_specs=specs,
        out_specs=out_specs or jax.tree.map(lambda _: VM, shape),
        compiler_params=pltpu.CompilerParams(vmem_limit_bytes=limit * 2**20),
        cost_estimate=pl.CostEstimate(flops=flops, bytes_accessed=moved, transcendentals=0),
    )(*args)


def eye(n):
    return (lax.broadcasted_iota(jnp.int32, (n, n), 0) == lax.broadcasted_iota(jnp.int32, (n, n), 1)).astype(BF)


def route_body(ids_ref, length_ref, quota_ref, compact_ref, match_ref, held_ref, chosen_ref, which_ref):
    n = ids_ref.shape[1]
    expert = lax.broadcasted_iota(jnp.int32, (EXPERTS, n), 0)
    chosen = jnp.zeros((EXPERTS, n), F32)
    for j in range(ids_ref.shape[0]):
        chosen = chosen + (ids_ref[j : j + 1, :] == expert).astype(F32)
    at = lax.broadcasted_iota(jnp.int32, (1, n), 1)
    picked = chosen * (at < length_ref[...]).astype(F32)
    down = lax.broadcasted_iota(jnp.int32, (n, n), 0)
    before = (down < lax.broadcasted_iota(jnp.int32, (n, n), 1)).astype(BF)
    order = dot(picked.astype(BF), before, 1, 0)
    quota = jnp.sum(eye(EXPERTS).astype(F32) * quota_ref[...].astype(F32), axis=1, keepdims=True)
    kept = picked * (order < quota).astype(F32)
    slot = lax.broadcasted_iota(jnp.int32, (SLOTS, n), 0).astype(F32)
    hits = [(order[e : e + 1, :] == slot).astype(F32) * kept[e : e + 1, :] for e in range(EXPERTS)]
    match = dot(eye(n), jnp.concatenate(hits, axis=0).astype(BF), 1, 1).astype(BF)
    used = jnp.max(kept, axis=0, keepdims=True)
    place = dot(jnp.broadcast_to(used, (8, n)).astype(BF), before, 1, 0)[0:1, :]
    compact = ((place == down.astype(F32)).astype(F32) * used).astype(BF)
    compact_ref[...] = compact
    match_ref[...] = match
    held_ref[...] = dot(compact, match, 1, 0).astype(BF)
    chosen_ref[...] = dot(compact, chosen.astype(BF), 1, 1)
    count = jnp.sum(used).astype(jnp.int32)
    which_ref[0] = sum((count > size).astype(jnp.int32) for size in SIZES[:-1])


def compact_body(compact_ref, tokens_ref, rows_ref, again_ref):
    rows = dot(compact_ref[...], tokens_ref[...], 1, 0).astype(BF)
    rows_ref[...] = rows
    again_ref[...] = rows


def blocks_of(rank, width):
    order = [rank // 4 * 4 + k for k in range(4)] + [rank ^ 4 ^ k for k in range(4)]
    return [pl.ds(pl.multiple_of(r * width, width), width) for r in order]


def pick(views, blocks, held, gain_ref, router_ref, out_ref, leave):
    n, width = views[0].shape
    squares = jnp.zeros((n, 1), F32)
    logits = jnp.zeros((n, EXPERTS), F32)
    for k, (view, cols) in enumerate(zip(views, blocks)):
        raw = view[...]
        out_ref[k] = dot(held, raw, 0, 0).astype(BF)
        leave(k)
        v = raw.astype(F32)
        squares = squares + jnp.sum(v * v, axis=1, keepdims=True)
        scaled = (v * gain_ref[:, cols].astype(F32)).astype(BF)
        logits = logits + dot(scaled, router_ref[:, cols], 1, 1)
    return squares, logits


def pick_first_body(own_ref, far_ref, held_ref, gain_ref, router_ref, out_ref, kept_far_ref, squares_ref, logits_ref, buffer, sems):
    n, width = far_ref.shape
    blocks = blocks_of(lax.axis_index("tensor"), width)[:5]
    views = [own_ref.at[k] for k in range(4)] + [far_ref]
    copies = []

    def leave(k):
        cols = slice(k * width, (k + 1) * width)
        copies.append(pltpu.make_async_copy(buffer.at[k], out_ref.at[:, cols], sems.at[k]))
        copies[k].start()

    squares, logits = pick(views, blocks, held_ref[0:n, :], gain_ref, router_ref, buffer, leave)
    kept_far_ref[0:n, :] = far_ref[...]
    squares_ref[0:n, :] = jnp.broadcast_to(squares, (n, squares_ref.shape[1]))
    logits_ref[0:n, :] = logits
    for copy in copies:
        copy.wait()


def pick_second_body(
    a_ref, b_ref, c_ref, held_ref, gain_ref, router_ref, squares_ref, logits_ref, match_ref, chosen_ref,
    out_ref, high_ref, low_ref, buffer, sems,
):
    n, width = a_ref.shape
    blocks = blocks_of(lax.axis_index("tensor"), width)[5:]
    held = held_ref[0:n, :]
    copies = []

    def leave(k):
        cols = slice(k * width, (k + 1) * width)
        copies.append(pltpu.make_async_copy(buffer.at[k], out_ref.at[:, cols], sems.at[k]))
        copies[k].start()

    squares, logits = pick([a_ref, b_ref, c_ref], blocks, held, gain_ref, router_ref, buffer, leave)
    inverse = lax.rsqrt((squares + squares_ref[0:n, 0:1]) / (8 * width) + norm_eps)
    chosen = chosen_ref[0:n, :]
    powered = jnp.exp((logits + logits_ref[0:n, :]) * inverse) * chosen
    weight = powered / (jnp.sum(powered, axis=1, keepdims=True) + (1.0 - jnp.max(chosen, axis=1, keepdims=True)))
    slots = held.shape[1]
    owner = (
        lax.broadcasted_iota(jnp.int32, (EXPERTS, slots), 1) // SLOTS
        == lax.broadcasted_iota(jnp.int32, (EXPERTS, slots), 0)
    ).astype(BF)
    spread = jnp.zeros((n, slots), F32)
    for _ in range(3):
        piece = weight.astype(BF)
        spread = spread + dot(piece, owner, 1, 0)
        weight = weight - piece.astype(F32)
    row = jnp.sum(spread * held.astype(F32), axis=0, keepdims=True)
    value = match_ref[...].astype(F32) * row
    high = value.astype(BF)
    high_ref[...] = high
    low_ref[...] = (value - high.astype(F32)).astype(BF)
    for copy in copies:
        copy.wait()


def partial_products(rows_ref, gain_ref, blocks, weights):
    rows = rows_ref.shape[0]
    squares = jnp.zeros((rows, 1), F32)
    gate = up = 0.0
    for k, cols in enumerate(blocks):
        width = rows_ref.shape[1] // len(blocks)
        v = rows_ref[:, k * width : (k + 1) * width].astype(F32)
        squares = squares + jnp.sum(v * v, axis=1, keepdims=True)
        scaled = (v * gain_ref[:, cols].astype(F32)).astype(BF)
        gate_part, up_part = weights(k)
        gate = gate + dot(gate_part, scaled, 1, 1)
        up = up + dot(up_part, scaled, 1, 1)
    return gate, up, jnp.broadcast_to(squares, (rows, 128)).T[0:1, :]


def expand_first_body(
    rows_ref, gain_ref, gate_ref, up_ref,
    parts_ref, gate_rest, up_rest, gate_buf, up_buf, sems,
):
    rank = lax.axis_index("tensor")
    now, _, width = gate_buf.shape
    blocks = blocks_of(rank, width)
    copies = []
    for k, cols in enumerate(blocks):
        targets = (gate_buf, up_buf) if k < now else (gate_rest, up_rest)
        at = k if k < now else k - now
        pair = [
            pltpu.make_async_copy(source.at[:, cols], target.at[at], sems.at[i, k])
            for i, (source, target) in enumerate(zip((gate_ref, up_ref), targets))
        ]
        for copy in pair:
            copy.start()
        copies.append(pair)

    def weights(k):
        for copy in copies[k]:
            copy.wait()
        return gate_buf[k], up_buf[k]

    gate, up, squares = partial_products(rows_ref, gain_ref, blocks[:now], weights)
    hid, rows = gate.shape
    parts_ref[0:hid, :] = gate
    parts_ref[hid : 2 * hid, :] = up
    parts_ref[2 * hid :, :] = jnp.broadcast_to(squares, (8, rows))
    for pair in copies[now:]:
        for copy in pair:
            copy.wait()


def expand_second_body(rows_ref, parts_hbm, gain_ref, gate_rest, up_rest, out_ref, copies_ref, parts_ref, sem):
    rank = lax.axis_index("tensor")
    parts, hid, width = gate_rest.shape
    copy = pltpu.make_async_copy(parts_hbm, parts_ref, sem)
    copy.start()
    blocks = blocks_of(rank, width)[8 - parts :]
    gate, up, squares = partial_products(
        rows_ref, gain_ref, blocks, lambda k: (gate_rest[k], up_rest[k])
    )
    copy.wait()
    inverse = lax.rsqrt((squares + parts_ref[2 * hid : 2 * hid + 1, :]) / (8 * width) + norm_eps)
    gate = (gate + parts_ref[0:hid, :]) * inverse
    up = (up + parts_ref[hid : 2 * hid, :]) * inverse
    hidden = (gate / (1.0 + jnp.exp(-gate)) * up).astype(BF)
    out_ref[...] = hidden
    for k in range(4):
        copies_ref[k] = hidden


def contract_body(first_ref, second_ref, down_ref, out_ref):
    parts, hid, _ = first_ref.shape
    side = lax.axis_index("tensor") // parts
    total = jnp.zeros(out_ref.shape, F32)
    for ref, half in ((first_ref, side), (second_ref, 1 - side)):
        for k in range(parts):
            rows = pl.ds(pl.multiple_of((half * parts + k) * hid, hid), hid)
            total = total + dot(ref[k], down_ref[rows, :], 0, 0)
    out_ref[...] = total.astype(BF)


def mix_body(high_ref, low_ref, reply_ref, tokens_ref, out_ref):
    mixed = dot(high_ref[...], reply_ref[...], 1, 0) + dot(low_ref[...], reply_ref[...], 1, 0)
    out_ref[...] = (tokens_ref[...].astype(F32) + mixed).astype(BF)


def fours(copies):
    return lax.all_to_all(copies, "tensor", 0, 0, axis_index_groups=FOURS)


def to_fours(shard):
    return fours(jnp.broadcast_to(shard[None], (4,) + shard.shape))


def to_fours_apart(rows, size, always):
    shape = (4, size) + rows.shape[1:]
    return lax.cond(always, lambda x: to_fours(x[:size]), lambda x: jnp.zeros(shape, x.dtype), rows)


def along(shard, by):
    return lax.ppermute(shard, "tensor", [(i, i ^ by) for i in range(8)])


def over_dp(rows):
    n, width = rows.shape
    return lax.all_to_all(rows.reshape(EXPERTS, n // EXPERTS, width), "dp", 0, 0).reshape(n, width)


def on_device(
    hidden_state_matrix,
    specialist_choice_ids,
    seat_quota_per_specialist,
    candidate_active_extent,
    normalizer_gain_vector,
    dispatcher_matrix,
    gating_matrices,
    expanding_matrices,
    contracting_matrices,
):
    tokens = hidden_state_matrix[0]
    ids = specialist_choice_ids[0].T
    gain = normalizer_gain_vector
    router = dispatcher_matrix[0]
    w_gate = gating_matrices[0, 0]
    w_up = expanding_matrices[0, 0]
    w_down = contracting_matrices[0, 0]
    n, width = tokens.shape
    slots = EXPERTS * SLOTS
    hid = w_gate.shape[0]

    table = jax.ShapeDtypeStruct((n, slots), BF)
    compact, match, held, chosen, which = call(
        route_body,
        (
            jax.ShapeDtypeStruct((n, n), BF),
            table,
            table,
            jax.ShapeDtypeStruct((n, EXPERTS), F32),
            jax.ShapeDtypeStruct((1,), jnp.int32),
        ),
        [VM] * 3,
        (ids, candidate_active_extent, seat_quota_per_specialist),
        out_specs=(VM,) * 4 + (SM,),
        limit=16,
    )
    packed = jax.ShapeDtypeStruct((n, width), BF)
    rows, again = call(compact_body, (packed, packed), [VM] * 2, (compact, tokens), limit=16)

    def first_part(size):
        def run(which, rows, again, held, gain, router):
            far = along(rows[:size], 4)
            return call(
                pick_first_body,
                (
                    jax.ShapeDtypeStruct((slots, 5 * width), BF),
                    jax.ShapeDtypeStruct((n, width), BF),
                    jax.ShapeDtypeStruct((n, 128), F32),
                    jax.ShapeDtypeStruct((n, EXPERTS), F32),
                ),
                [VM] * 5,
                (to_fours_apart(again, size, which[0] < len(SIZES)), far, held, gain, router),
                [pltpu.VMEM((5, slots, width), BF), pltpu.SemaphoreType.DMA((5,))],
                out_specs=(HB, VM, VM, VM),
                limit=16,
            )

        return run

    def second_part(size):
        def run(far, held, gain, router, squares, logits, match, chosen):
            rest = [along(far[:size], by) for by in (1, 2, 3)]
            return call(
                pick_second_body,
                (jax.ShapeDtypeStruct((slots, 3 * width), BF), table, table),
                [VM] * 10,
                (*rest, held, gain, router, squares, logits, match, chosen),
                [pltpu.VMEM((3, slots, width), BF), pltpu.SemaphoreType.DMA((3,))],
                out_specs=(HB, VM, VM),
                limit=16,
            )

        return run

    first, far, squares, logits = lax.switch(
        which[0], [first_part(size) for size in SIZES], which, rows, again, held, gain, router
    )
    first_rows = over_dp(first)
    second, high, low = lax.switch(
        which[0], [second_part(size) for size in SIZES], far, held, gain, router, squares, logits, match, chosen
    )
    first_rows, second = lax.optimization_barrier((first_rows, second))
    second_rows = over_dp(second)
    parts = jax.ShapeDtypeStruct((2 * hid + 8, slots), F32)
    weights = jax.ShapeDtypeStruct((3, hid, width), BF)
    parts, gate_rest, up_rest = call(
        expand_first_body,
        (parts, weights, weights),
        [VM] * 2 + [HB] * 2,
        (first_rows, gain, w_gate, w_up),
        [pltpu.VMEM((5, hid, width), BF)] * 2 + [pltpu.SemaphoreType.DMA((2, 8))],
        limit=16,
    )
    hidden, copies = call(
        expand_second_body,
        (jax.ShapeDtypeStruct((hid, slots), BF), jax.ShapeDtypeStruct((4, hid, slots), BF)),
        [VM, HB, VM, VM, VM],
        (second_rows, parts, gain, gate_rest, up_rest),
        [pltpu.VMEM((2 * hid + 8, slots), F32), pltpu.SemaphoreType.DMA],
        limit=16,
    )
    hidden_other = along(hidden, 4)
    hidden_first = fours(copies)
    hidden_second = to_fours(hidden_other)
    reply = call(
        contract_body,
        jax.ShapeDtypeStruct((slots, width), BF),
        [VM] * 3,
        (hidden_first, hidden_second, w_down),
    )
    returned = over_dp(reply)
    layer_out = call(
        mix_body, jax.ShapeDtypeStruct((n, width), BF), [VM] * 4, (high, low, returned, tokens)
    )
    count = lax.axis_size("section")
    handed = lax.ppermute(layer_out, "section", [(i, (i + 1) % count) for i in range(count)])
    return handed[None]


def solution(mesh):
    return jax.shard_map(
        on_device,
        mesh=mesh,
        in_specs=(
            P("section", "dp", "tensor"),
            P("section", "dp", None),
            P("section", None),
            P("section", "dp"),
            P("section", None),
            P("section", None, None),
            P("section", "dp", "tensor", None),
            P("section", "dp", "tensor", None),
            P("section", "dp", None, "tensor"),
        ),
        out_specs=P("section", "dp", "tensor"),
        check_vma=False,
    )
```
